512 devices in a mesh: feat: 32 (over y, x), samp: 8 (over z), rep: 2 (over core).
Axes of the slice: x: 4, y: 8, z: 8, core: 2. Of those that a mesh axis runs over, the one named last changes fastest.
Arguments:
- tiles: bfloat16 [32, 16, 32, 128, 256], P('feat', ('samp', 'rep')), may hold values from -0.25 to 0.25
- tile_block: int32 [32, 16, 32], P('feat', ('samp', 'rep')), may hold values from -1 to 63, as said below
- tile_row: int32 [32, 16, 32], P('feat', ('samp', 'rep')), may hold values from 0 to 31
- labels: int32 [65536], P(('samp', 'rep')), may hold values 0 or 1
- weights: float32 [524288], P('feat')
- hess_inv: float32 [2048, 256, 256], P(('feat', 'samp', 'rep'))
- order: int32 [32, 64], P('feat'), may hold values from 0 to 63, each once within a row
- sweeps: int32 [2048], P('feat'), may hold values from 1 to 3
Outputs:
- direction: float32 [524288], P(('feat', 'samp', 'rep'))
- margin_change: float32 [65536], P(('samp', 'rep'))
- decrease: float32 [1], replicated
The draws below stay inside these ranges and needn't reach their ends.
Inputs may be any that keep to these rules, and one draw needn't show every extreme that they name: `tile_block`: in every group the live slots come first and the rest hold -1; at least half of the 32 slots of every group are live, and some group has all live.
All inputs are finite; a program needn't handle non-finite values. No bound on the sum of `labels` on one device may be relied on, other than what follows from the above.
Results may differ from the reference program's by a relative error of at most 0.029.
Values may be sent and summed in bfloat16 or wider, within the bound.
A program may use at most 128 MiB of HBM per device.

```python
import jax
import jax.numpy as jnp
from jax import lax

BLOCK = 256
BLK_DEV = 64
TR = 128
CAP = 32
R_DEV = 4096
SWEEPS = 3
SEGMENTS = 2
ROWS = 65536
N_FEAT = 32
N_SAMP = 8
N_REP = 2


def draw_tile_block(key, part):
    key = jax.random.fold_in(key, 11)
    key_ids, key_live = jax.random.split(key)
    groups = N_SAMP * N_REP
    blocks = jax.random.randint(key_ids, (N_FEAT, groups, CAP), 0, BLK_DEV)
    live_count = jax.random.randint(key_live, (N_FEAT, groups, 1), CAP // 2, CAP + 1)
    first_group = (jnp.arange(N_FEAT)[:, None, None] == 0) & (jnp.arange(groups)[None, :, None] == 0)
    live_count = jnp.where(first_group, CAP, live_count)
    first_slot = first_group & (jnp.arange(CAP)[None, None, :] == 0)
    blocks = jnp.where(first_slot, BLK_DEV - 1, blocks)
    return jnp.where(jnp.arange(CAP)[None, None, :] < live_count, blocks, -1).astype(jnp.int32)


def draw_tile_row(key, part):
    key = jax.random.fold_in(key, 12)
    groups = N_SAMP * N_REP
    row_ids = jax.random.randint(key, (N_FEAT, groups, CAP), 0, R_DEV // TR)
    first_slot = (jnp.arange(N_FEAT)[:, None, None] == 0) & (jnp.arange(groups)[None, :, None] == 0) & (jnp.arange(CAP)[None, None, :] == 0)
    return jnp.where(first_slot, R_DEV // TR - 1, row_ids).astype(jnp.int32)


def draw_weights(key, part):
    key = jax.random.fold_in(key, 13)
    key_vals, key_keep = jax.random.split(key)
    total = BLK_DEV * N_FEAT * BLOCK
    values = jax.random.normal(key_vals, (total,), jnp.float32) * 0.25
    keep = jax.random.uniform(key_keep, (total,), jnp.float32) < 0.5
    return jnp.where(keep, values, 0.0).astype(jnp.float32)


def draw_hess_inv(key, part):
    key = jax.random.fold_in(key, 14)
    key_off, key_diag = jax.random.split(key)
    count = BLK_DEV * N_FEAT
    off_part = jax.random.normal(key_off, (count, BLOCK, BLOCK), jnp.float32) * (0.3 * BLOCK ** (-0.5))
    diag_part = jax.random.uniform(key_diag, (count, BLOCK, 1), jnp.float32, 0.5, 1.5)
    on_diag = jnp.arange(BLOCK)[:, None] == jnp.arange(BLOCK)[None, :]
    return jnp.where(on_diag[None, :, :], diag_part, off_part).astype(jnp.float32)


def draw_sweeps(key, part):
    key = jax.random.fold_in(key, 15)
    count = BLK_DEV * N_FEAT
    counts = jax.random.randint(key, (count,), 1, SWEEPS + 1)
    index = jnp.arange(count)
    counts = jnp.where(index == 0, SWEEPS, counts)
    counts = jnp.where(index == 1, 1, counts)
    return counts.astype(jnp.int32)


def set_ends(entries, own_key, low, top_value):
    longest = entries.shape.index(max(entries.shape))
    spots = []
    for shift in (0, 1):
        where = [jax.random.randint(jax.random.fold_in(own_key, axis), (), 0, length) for axis, length in enumerate(entries.shape)]
        where[longest] = (where[longest] + shift) % entries.shape[longest]
        spots.append(tuple(where))
    return entries.at[spots[0]].set(low).at[spots[1]].set(top_value)


def block_scale(stream_key, shape, shards, low, high):
    loudness = 1.0
    for axis_at, shards_of in shards:
        heights = jax.random.uniform(jax.random.fold_in(jax.random.fold_in(stream_key, 6), axis_at), (shards_of,), jnp.float32, low / len(shards), high / len(shards))
        loudness = loudness * jnp.repeat(jnp.exp(heights), shape[axis_at] // shards_of).reshape((-1,) + (1,) * (len(shape) - 1 - axis_at))
    return loudness


def normal_values(rng, shape, spread, reach, pieces=(), kind=jnp.bfloat16):
    level = block_scale(rng, shape, pieces, -0.22, 0.18) if pieces else 1.0
    array = jax.random.normal(rng, shape, jnp.float32) * spread * level
    return jnp.minimum(jnp.maximum(array, -reach), reach).astype(kind)


def setup_inputs(seed: int = 0) -> dict:
    key_list = jax.random.split(jax.random.key(seed), 9)
    tiles = normal_values(key_list[0], (N_FEAT, N_SAMP * N_REP, CAP, TR, BLOCK), (BLOCK * N_FEAT // 16) ** -0.5, 0.25, ((0, 32), (1, 16)))
    tile_block = draw_tile_block(jax.random.fold_in(key_list[8], 71), 0)
    tile_row = draw_tile_row(jax.random.fold_in(key_list[8], 71), 0)
    labels = set_ends((jax.random.randint(key_list[3], (ROWS,), 0, 2) < 1).astype(jnp.int32), jax.random.fold_in(key_list[3], 1), 0, 1)
    weights = draw_weights(jax.random.fold_in(key_list[8], 71), 0)
    hess_inv = draw_hess_inv(jax.random.fold_in(key_list[8], 71), 0)
    order = jax.vmap(lambda own: jax.random.permutation(own, BLK_DEV))(jax.random.split(key_list[6], N_FEAT)).reshape((N_FEAT, BLK_DEV)).astype(jnp.int32)
    sweeps = draw_sweeps(jax.random.fold_in(key_list[8], 71), 0)
    return {"tiles": tiles, "tile_block": tile_block, "tile_row": tile_row, "labels": labels, "weights": weights, "hess_inv": hess_inv, "order": order, "sweeps": sweeps}


penalty = 0.05
ridge_term = 0.1


def margin_product(tiles, tile_block, tile_row, block_vectors):
    row_count = R_DEV // TR

    def one_group(group_args):
        group_tiles, group_block, group_row, group_vec = group_args
        block_hot = (group_block[:, :, None] == jnp.arange(BLK_DEV)[None, None, :]).astype(jnp.float32)
        row_hot = (group_row[:, :, None] == jnp.arange(row_count)[None, None, :]).astype(jnp.float32)
        chosen = jnp.einsum('scb,bk->sck', block_hot, group_vec.astype(jnp.float32), precision=lax.Precision.HIGHEST)
        partial_value = jnp.einsum('sctk,sck->sct', group_tiles.astype(jnp.float32), chosen, precision=lax.Precision.HIGHEST)
        return jnp.einsum('sct,scr->srt', partial_value, row_hot, precision=lax.Precision.HIGHEST)

    per_group = lax.map(one_group, (tiles, tile_block, tile_row, block_vectors))
    return jnp.sum(per_group, axis=0).reshape(-1)


def gradient_product(tiles, tile_block, tile_row, rows_bf):
    row_count = R_DEV // TR
    rows_full = rows_bf.astype(jnp.float32).reshape(N_SAMP * N_REP, row_count, TR)

    def one_group(group_args):
        group_tiles, group_block, group_row = group_args
        block_hot = (group_block[:, :, None] == jnp.arange(BLK_DEV)[None, None, :]).astype(jnp.float32)
        row_hot = (group_row[:, :, None] == jnp.arange(row_count)[None, None, :]).astype(jnp.float32)
        picked = jnp.einsum('scr,srt->sct', row_hot, rows_full, precision=lax.Precision.HIGHEST)
        contrib = jnp.einsum('sctk,sct->sck', group_tiles.astype(jnp.float32), picked, precision=lax.Precision.HIGHEST)
        return jnp.einsum('sck,scb->bk', contrib, block_hot, precision=lax.Precision.HIGHEST)

    return lax.map(one_group, (tiles, tile_block, tile_row)).reshape(N_FEAT * BLK_DEV, BLOCK)


def reference(tiles, tile_block, tile_row, labels, weights, hess_inv, order, sweeps):
    flat_w = weights.reshape(N_FEAT * BLK_DEV, BLOCK)
    margins = margin_product(tiles, tile_block, tile_row, weights.astype(jnp.bfloat16).reshape(N_FEAT, BLK_DEV, BLOCK))
    probability = jax.nn.sigmoid(margins)
    curvature = probability * (1.0 - probability)
    resid_bf = (probability - labels.astype(jnp.float32)).astype(jnp.bfloat16)
    gradient = gradient_product(tiles, tile_block, tile_row, resid_bf)
    threshold = penalty * jnp.diagonal(hess_inv, axis1=1, axis2=2)
    matches = order[:, :, None] == jnp.arange(BLK_DEV)[None, None, :]
    positions = jnp.sum(jnp.where(matches, jnp.arange(BLK_DEV)[None, :, None], 0), axis=1)
    segment_of = (positions // (BLK_DEV // SEGMENTS)).reshape(-1)
    direction = jnp.zeros((N_FEAT * BLK_DEV, BLOCK), jnp.float32)
    change = jnp.zeros((R_DEV * N_SAMP * N_REP,), jnp.float32)
    for sweep_index in range(SWEEPS):
        for segment_index in range(SEGMENTS):
            scaled = (curvature * change).astype(jnp.bfloat16)
            hess_part = gradient_product(tiles, tile_block, tile_row, scaled)
            model_grad = gradient + hess_part + ridge_term * direction
            trial_point = flat_w + direction - jnp.einsum('bij,bj->bi', hess_inv, model_grad, precision=lax.Precision.HIGHEST)
            shrunk = jnp.sign(trial_point) * jnp.maximum(jnp.abs(trial_point) - threshold, 0.0)
            active = (segment_of == segment_index) & (sweep_index < sweeps)
            step_delta = jnp.where(active[:, None], shrunk - flat_w - direction, 0.0)
            direction = direction + step_delta
            step_bf = step_delta.astype(jnp.bfloat16).reshape(N_FEAT, BLK_DEV, BLOCK)
            change = change + margin_product(tiles, tile_block, tile_row, step_bf)
    linear = jnp.sum(gradient * direction) + 0.5 * ridge_term * jnp.sum(direction * direction)
    linear = linear + penalty * jnp.sum(jnp.abs(flat_w + direction) - jnp.abs(flat_w))
    quadratic = 0.5 * jnp.sum(curvature * change * change)
    decrease = (linear + quadratic).reshape(1)
    return direction.reshape(-1), change, decrease
```

```python
import functools

import jax
import jax.numpy as jnp
from jax import lax
from jax.experimental import pallas as pl
from jax.experimental.pallas import tpu as pltpu
from jax.sharding import PartitionSpec as P

SWEEPS = 3
SEGMENTS = 2
ROUNDS = SWEEPS * SEGMENTS

NX = 4
NY = 8
NM = 16
SLOTS = 32
TILE_ROWS = 128
WIDTH = 256
HALF = 128
GROUPS = 32
BLOCKS = 64
OWNED = 4

penalty = 0.05
ridge_term = 0.1

MESH = pl.DeviceIdType.MESH
F32 = jnp.float32
BF16 = jnp.bfloat16


def far_first(count, chips):
    per = count // chips
    return sorted(range(1, count), key=lambda j: -min(j // per, chips - j // per))


def iota(shape, dim):
    return lax.broadcasted_iota(jnp.int32, shape, dim)


def body(
    tile_block,
    tile_row,
    order,
    sweeps,
    tiles,
    labels,
    weights,
    hess,
    dir_out,
    change_out,
    dec_out,
    tiles_t,
    hess_t,
    vecs,
    rows,
    q_buf,
    p_buf,
    thr,
    w_own,
    grad,
    direc,
    curv,
    x_buf,
    y_buf,
    rs_out,
    rs_in,
    ag_buf,
    lx_buf,
    ly_buf,
    lz_buf,
    x_send,
    x_recv,
    y_send,
    y_recv,
    z_send,
    z_recv,
    l_send,
    l_recv,
):
    f, s, r = lax.axis_index("feat"), lax.axis_index("samp"), lax.axis_index("rep")
    me_x, me_y = f % NX, f // NX
    me = s * 2 + r

    def x_dev(j):
        return (me_y * NX + (me_x + j) % NX, s, r)

    def y_dev(j):
        return ((me_y + j) % NY * NX + me_x, s, r)

    def z_dev(j):
        return (f, (s + j // 2) % 8, r ^ (j % 2))

    barrier = pltpu.get_barrier_semaphore()
    for dev, count in ((x_dev, NX), (y_dev, NY), (z_dev, NM)):
        for j in range(1, count):
            pl.semaphore_signal(barrier, inc=1, device_id=dev(j), device_id_type=MESH)

    for m in range(NM):
        vecs[8 * m : 8 * m + 4] = weights[pl.ds(8 * m, 4, stride=2)]
        vecs[8 * m + 4 : 8 * m + 8] = weights[pl.ds(8 * m + 1, 4, stride=2)]
    w_own[...] = vecs[pl.ds(pl.multiple_of(me * 8, 8), 8)]
    direc[...] = jnp.zeros((8, HALF), F32)
    change_out[...] = jnp.zeros((GROUPS, TILE_ROWS), F32)

    def flip_tile(c, carry):
        tiles_t[c] = tiles[c].T
        return carry

    lax.fori_loop(0, SLOTS, flip_tile, 0, unroll=4)

    def flip_hess(i, carry):
        block = hess[i]
        flipped = block.T
        high = flipped.astype(BF16)
        hess_t[i] = high
        hess_t[OWNED + i] = (flipped - high.astype(F32)).astype(BF16)
        on_diag = iota((WIDTH, WIDTH), 0) == iota((WIDTH, WIDTH), 1)
        diagonal = jnp.sum(jnp.where(on_diag, block, 0.0), axis=0, keepdims=True)
        thr[pl.ds(i, 1)] = penalty * diagonal[:, :HALF]
        thr[pl.ds(OWNED + i, 1)] = penalty * diagonal[:, HALF:]
        return carry

    lax.fori_loop(0, OWNED, flip_hess, 0)

    sub = iota((8, HALF), 0) % OWNED
    first_half = jnp.zeros((8, HALF), jnp.int32)
    limit = jnp.zeros((8, HALF), jnp.int32)
    for i in range(OWNED):
        own_block = me * OWNED + i
        found = jnp.int32(0)
        for p in range(BLOCKS // SEGMENTS):
            found = found + jnp.where(order[0, p] == own_block, 1, 0)
        first_half = jnp.where(sub == i, found, first_half)
        limit = jnp.where(sub == i, sweeps[own_block], limit)
    own_segment = 1 - first_half

    pl.semaphore_wait(barrier, NX + NY + NM - 3)

    row_iota = iota((GROUPS, HALF), 0)
    block_iota = iota((BLOCKS, TILE_ROWS), 0)

    def forward():
        def fill(c, carry):
            b = tile_block[0, 0, c]
            live = b >= 0
            b = jnp.maximum(b, 0)
            at = 8 * (b // 4) + b % 4
            group = jnp.where(live, tile_row[0, 0, c], -1)
            hot = row_iota == group
            left = jnp.where(hot, vecs[pl.ds(at, 1)], 0.0).astype(BF16)
            right = jnp.where(hot, vecs[pl.ds(at + 4, 1)], 0.0).astype(BF16)
            base = pl.multiple_of(c * WIDTH, WIDTH)
            q_buf[:, pl.ds(base, HALF)] = left
            q_buf[:, pl.ds(base + HALF, HALF)] = right
            return carry

        lax.fori_loop(0, SLOTS, fill, 0, unroll=True)
        flipped = tiles_t[...].reshape(SLOTS * WIDTH, TILE_ROWS)
        return jnp.dot(q_buf[...], flipped, preferred_element_type=F32)

    def backward():
        def fill(c, carry):
            b = tile_block[0, 0, c]
            picked = rows[pl.ds(tile_row[0, 0, c], 1)]
            base = pl.multiple_of(c * TILE_ROWS, TILE_ROWS)
            p_buf[:, pl.ds(base, TILE_ROWS)] = jnp.where(block_iota == b, picked, 0.0).astype(BF16)
            return carry

        lax.fori_loop(0, SLOTS, fill, 0, unroll=True)
        flat = tiles[...].reshape(SLOTS * TILE_ROWS, WIDTH)
        return jnp.dot(p_buf[...], flat, preferred_element_type=F32)

    def send(src, dst, send_sem, recv_sem, dev):
        pltpu.make_async_remote_copy(
            src_ref=src,
            dst_ref=dst,
            send_sem=send_sem,
            recv_sem=recv_sem,
            device_id=dev,
            device_id_type=MESH,
        ).start()

    def drain(ref, sem):
        pltpu.make_async_copy(ref, ref, sem).wait()

    def line_start(buf, value, me_at, count, send_sem, recv_sem, dev):
        buf[me_at] = value
        for j in far_first(count, min(count, 8)):
            send(buf.at[me_at], buf.at[me_at], send_sem, recv_sem, dev(j))

    def line_finish(buf, count, send_sem, recv_sem):
        drain(buf.at[pl.ds(0, count - 1)], recv_sem)
        total = buf[0].astype(F32)
        for k in range(1, count):
            total = total + buf[k].astype(F32)
        drain(buf.at[pl.ds(0, count - 1)], send_sem)
        return total

    def reduce_rows(part, slot):
        xb, yb = x_buf.at[slot], y_buf.at[slot]
        xs, xr, ys, yr = x_send.at[slot], x_recv.at[slot], y_send.at[slot], y_recv.at[slot]
        line_start(xb, part.astype(BF16), me_x, NX, xs, xr, x_dev)
        total = line_finish(xb, NX, xs, xr)
        line_start(yb, total.astype(BF16), me_y, NY, ys, yr, y_dev)
        return line_finish(yb, NY, ys, yr)

    def one_round(t, carry):
        summed = reduce_rows(forward(), t % 2)

        @pl.when(t == 0)
        def _():
            prob = jax.nn.sigmoid(summed)
            curv[...] = prob * (1.0 - prob)
            rows[...] = prob - labels[...].astype(F32)

        @pl.when(t > 0)
        def _():
            change = change_out[...] + summed
            change_out[...] = change
            rows[...] = curv[...] * change

        contrib = backward()
        for m in range(NM):
            rs_out[m] = jnp.concatenate(
                [
                    contrib[OWNED * m : OWNED * (m + 1), :HALF],
                    contrib[OWNED * m : OWNED * (m + 1), HALF:],
                ],
                axis=0,
            )
        for j in far_first(NM, 8):
            dev = z_dev(j)
            send(rs_out.at[dev[1] * 2 + dev[2]], rs_in.at[j - 1], z_send.at[0], z_recv.at[0], dev)
        mine = rs_out[me]
        drain(rs_in, z_recv.at[0])
        for j in range(NM - 1):
            mine = mine + rs_in[j]
        drain(rs_in, z_send.at[0])

        @pl.when(t == 0)
        def _():
            grad[...] = mine

        direction = direc[...]
        model_grad = grad[...] + jnp.where(t > 0, mine, 0.0) + ridge_term * direction
        wide = jnp.concatenate([model_grad[:OWNED], model_grad[OWNED:]], axis=1)
        high = wide.astype(BF16).astype(F32)
        pair = jnp.concatenate([high, wide - high, jnp.zeros((8, WIDTH), F32)], axis=0)
        at = iota((16, WIDTH), 0)
        parts = [jnp.where(at % OWNED == i, pair, 0.0) for i in range(OWNED)]
        parts += [jnp.where(at == i, pair, 0.0) for i in range(OWNED)]
        spread = jnp.concatenate(parts, axis=1).astype(BF16)
        product = jnp.dot(
            spread, hess_t[...].reshape(2 * OWNED * WIDTH, WIDTH), preferred_element_type=F32
        )
        product = product[:OWNED] + product[OWNED : 2 * OWNED]
        newton = jnp.concatenate([product[:, :HALF], product[:, HALF:]], axis=0)
        weight = w_own[...]
        trial = weight + direction - newton
        size = jnp.maximum(jnp.abs(trial) - thr[...], 0.0)
        shrunk = jnp.where(trial > 0.0, size, jnp.where(trial < 0.0, -size, 0.0))
        active = (own_segment == t % SEGMENTS) & (t // SEGMENTS < limit)
        step = jnp.where(active, shrunk - weight - direction, 0.0)
        direc[...] = direction + step

        slot = ag_buf.at[pl.ds(pl.multiple_of(me * 8, 8), 8)]
        slot[...] = step
        for j in far_first(NM, 8):
            send(slot, slot, z_send.at[1], z_recv.at[1], z_dev(j))
        drain(ag_buf.at[pl.ds(0, 8 * (NM - 1))], z_recv.at[1])
        vecs[...] = ag_buf[...]
        drain(ag_buf.at[pl.ds(0, 8 * (NM - 1))], z_send.at[1])
        return carry

    lax.fori_loop(0, ROUNDS, one_round, 0)

    direction = direc[...]
    weight = w_own[...]
    linear = grad[...] * direction + 0.5 * ridge_term * direction * direction
    linear = linear + penalty * (jnp.abs(weight + direction) - jnp.abs(weight))
    line_start(lx_buf, linear, me_x, NX, l_send.at[0], l_recv.at[0], x_dev)
    part = forward()
    linear = line_finish(lx_buf, NX, l_send.at[0], l_recv.at[0])
    line_start(ly_buf, linear, me_y, NY, l_send.at[1], l_recv.at[1], y_dev)
    summed = reduce_rows(part, ROUNDS % 2)
    change = change_out[...] + summed
    linear = line_finish(ly_buf, NY, l_send.at[1], l_recv.at[1])
    quad = 0.5 * curv[...] * change * change
    for g in range(GROUPS // 8):
        linear = linear + quad[8 * g : 8 * g + 8]
    line_start(lz_buf, linear, me, NM, l_send.at[2], l_recv.at[2], z_dev)
    change_out[...] = change
    dir_out[pl.ds(0, OWNED, stride=2)] = direction[:OWNED]
    dir_out[pl.ds(1, OWNED, stride=2)] = direction[OWNED:]
    total = line_finish(lz_buf, NM, l_send.at[2], l_recv.at[2])
    dec_out[...] = jnp.sum(jnp.sum(total, axis=0, keepdims=True), axis=1, keepdims=True)


def on_device(tiles, tile_block, tile_row, labels, weights, hess_inv, order, sweeps):
    smem = pl.BlockSpec(memory_space=pltpu.SMEM)
    vmem = pl.BlockSpec(memory_space=pltpu.VMEM)
    dma = pltpu.SemaphoreType.DMA
    direction, change, decrease = pl.pallas_call(
        body,
        out_shape=(
            jax.ShapeDtypeStruct((8, HALF), F32),
            jax.ShapeDtypeStruct((GROUPS, TILE_ROWS), F32),
            jax.ShapeDtypeStruct((1, 1), F32),
        ),
        in_specs=[smem] * 4 + [vmem] * 4,
        out_specs=[vmem] * 3,
        scratch_shapes=[
            pltpu.VMEM((SLOTS, WIDTH, TILE_ROWS), BF16),
            pltpu.VMEM((2 * OWNED, WIDTH, WIDTH), BF16),
            pltpu.VMEM((8 * NM, HALF), F32),
            pltpu.VMEM((GROUPS, TILE_ROWS), F32),
            pltpu.VMEM((GROUPS, SLOTS * WIDTH), BF16),
            pltpu.VMEM((BLOCKS, SLOTS * TILE_ROWS), BF16),
            pltpu.VMEM((8, HALF), F32),
            pltpu.VMEM((8, HALF), F32),
            pltpu.VMEM((8, HALF), F32),
            pltpu.VMEM((8, HALF), F32),
            pltpu.VMEM((GROUPS, TILE_ROWS), F32),
            pltpu.VMEM((2, NX, GROUPS, TILE_ROWS), BF16),
            pltpu.VMEM((2, NY, GROUPS, TILE_ROWS), BF16),
            pltpu.VMEM((NM, 8, HALF), F32),
            pltpu.VMEM((NM - 1, 8, HALF), F32),
            pltpu.VMEM((8 * NM, HALF), F32),
            pltpu.VMEM((NX, 8, HALF), F32),
            pltpu.VMEM((NY, 8, HALF), F32),
            pltpu.VMEM((NM, 8, HALF), F32),
            dma((2,)),
            dma((2,)),
            dma((2,)),
            dma((2,)),
            dma((2,)),
            dma((2,)),
            dma((3,)),
            dma((3,)),
        ],
        compiler_params=pltpu.CompilerParams(
            collective_id=0, has_side_effects=True, vmem_limit_bytes=40 * 1024 * 1024
        ),
    )(
        tile_block,
        tile_row,
        order,
        sweeps,
        tiles.reshape(SLOTS, TILE_ROWS, WIDTH),
        labels.reshape(GROUPS, TILE_ROWS),
        weights.reshape(2 * BLOCKS, HALF),
        hess_inv,
    )
    return direction.reshape(-1), change.reshape(-1), decrease.reshape(1)


def solution(mesh):
    in_specs = (
        P("feat", ("samp", "rep"), None, None, None),
        P("feat", ("samp", "rep"), None),
        P("feat", ("samp", "rep"), None),
        P(("samp", "rep")),
        P("feat"),
        P(("feat", "samp", "rep"), None, None),
        P("feat", None),
        P("feat"),
    )
    out_specs = (P(("feat", "samp", "rep")), P(("samp", "rep")), P())
    return jax.shard_map(
        on_device, mesh=mesh, in_specs=in_specs, out_specs=out_specs, check_vma=False
    )
```

```python
import functools

import jax
import jax.numpy as jnp
from jax import lax
from jax.experimental import pallas as pl
from jax.experimental.pallas import tpu as pltpu
from jax.sharding import PartitionSpec as P

SWEEPS = 3
SEGMENTS = 2
ROUNDS = SWEEPS * SEGMENTS

NX = 4
NY = 8
NZ = 8
NM = 16
SLOTS = 32
TILE_ROWS = 128
WIDTH = 256
HALF = 128
GROUPS = 32
BLOCKS = 64
OWNED = 8
SHARE = 4
PIECES = 4

penalty = 0.05
ridge_term = 0.1

MESH = pl.DeviceIdType.MESH
F32 = jnp.float32
BF16 = jnp.bfloat16


def far_first(count, chips):
    per = count // chips
    return sorted(range(1, count), key=lambda j: -min(j // per, chips - j // per))


def iota(shape, dim):
    return lax.broadcasted_iota(jnp.int32, shape, dim)


def body(
    tile_block_hbm,
    tile_row_hbm,
    order_hbm,
    sweeps_hbm,
    tiles_hbm,
    labels_hbm,
    weights_hbm,
    hess_hbm,
    dir_out,
    change_out,
    dec_out,
    tile_block,
    tile_row,
    order,
    sweeps,
    tiles,
    labels,
    weights,
    hess,
    tiles_t,
    hess_t,
    vecs,
    rows,
    q_buf,
    p_buf,
    thr,
    w_own,
    grad,
    direc,
    segment,
    limit,
    curv,
    x_buf,
    y_buf,
    rs_out,
    rs_in,
    ag_buf,
    lx_buf,
    ly_buf,
    lz_buf,
    x_send,
    x_recv,
    y_send,
    y_recv,
    z_send,
    z_recv,
    l_send,
    l_recv,
    h_send,
    h_recv,
    load_sem,
):
    f, s, r = lax.axis_index("feat"), lax.axis_index("samp"), lax.axis_index("rep")
    me_x, me_y = f % NX, f // NX
    me = s * 2 + r

    def x_dev(j):
        return (me_y * NX + (me_x + j) % NX, s, r)

    def y_dev(j):
        return ((me_y + j) % NY * NX + me_x, s, r)

    def z_dev(j):
        return (f, (s + j // 2) % NZ, r ^ (j % 2))

    def z_same(j):
        return (f, (s + j) % NZ, r)

    def load(src, dst, k):
        return pltpu.make_async_copy(src, dst, load_sem.at[k])

    loads = [
        load(tile_block_hbm, tile_block, 0),
        load(tile_row_hbm, tile_row, 1),
        load(weights_hbm, weights, 2),
    ]
    per_piece = SLOTS // PIECES
    pieces = [
        load(
            tiles_hbm.at[pl.ds(k * per_piece, per_piece)],
            tiles.at[pl.ds(k * per_piece, per_piece)],
            3 + k,
        )
        for k in range(PIECES)
    ]
    later = [
        load(hess_hbm, hess, 3 + PIECES),
        load(labels_hbm, labels, 4 + PIECES),
        load(order_hbm, order, 5 + PIECES),
        load(sweeps_hbm, sweeps, 6 + PIECES),
    ]
    for copy in loads + pieces + later:
        copy.start()

    barrier = pltpu.get_barrier_semaphore()
    for dev, count in ((x_dev, NX), (y_dev, NY), (z_dev, NM)):
        for j in range(1, count):
            pl.semaphore_signal(barrier, inc=1, device_id=dev(j), device_id_type=MESH)

    row_iota = iota((GROUPS, HALF), 0)
    block_iota = iota((BLOCKS, TILE_ROWS), 0)

    def fill_forward():
        def fill(c, carry):
            b = tile_block[0, 0, c]
            live = b >= 0
            b = jnp.maximum(b, 0)
            at = 2 * OWNED * (b // OWNED) + b % OWNED
            group = jnp.where(live, tile_row[0, 0, c], -1)
            hot = row_iota == group
            left = jnp.where(hot, vecs[pl.ds(at, 1)], 0.0).astype(BF16)
            right = jnp.where(hot, vecs[pl.ds(at + OWNED, 1)], 0.0).astype(BF16)
            base = pl.multiple_of(c * WIDTH, WIDTH)
            q_buf[:, pl.ds(base, HALF)] = left
            q_buf[:, pl.ds(base + HALF, HALF)] = right
            return carry

        lax.fori_loop(0, SLOTS, fill, 0, unroll=True)

    def forward():
        flipped = tiles_t[...].reshape(SLOTS * WIDTH, TILE_ROWS)
        return jnp.dot(q_buf[...], flipped, preferred_element_type=F32)

    def backward():
        def fill(c, carry):
            b = tile_block[0, 0, c]
            picked = rows[pl.ds(tile_row[0, 0, c], 1)]
            base = pl.multiple_of(c * TILE_ROWS, TILE_ROWS)
            p_buf[:, pl.ds(base, TILE_ROWS)] = jnp.where(block_iota == b, picked, 0.0).astype(BF16)
            return carry

        lax.fori_loop(0, SLOTS, fill, 0, unroll=True)
        flat = tiles[...].reshape(SLOTS * TILE_ROWS, WIDTH)
        return jnp.dot(p_buf[...], flat, preferred_element_type=F32)

    def remote(src, dst, send_sem, recv_sem, dev):
        return pltpu.make_async_remote_copy(
            src_ref=src,
            dst_ref=dst,
            send_sem=send_sem,
            recv_sem=recv_sem,
            device_id=dev,
            device_id_type=MESH,
        )

    def send(src, dst, send_sem, recv_sem, dev):
        remote(src, dst, send_sem, recv_sem, dev).start()

    def drain(ref, sem):
        pltpu.make_async_copy(ref, ref, sem).wait()

    def line_start(buf, value, me_at, count, send_sem, recv_sem, dev):
        buf[me_at] = value
        for j in far_first(count, min(count, 8)):
            send(buf.at[me_at], buf.at[me_at], send_sem, recv_sem, dev(j))

    def line_finish(buf, count, send_sem, recv_sem):
        drain(buf.at[pl.ds(0, count - 1)], recv_sem)
        total = buf[0].astype(F32)
        for k in range(1, count):
            total = total + buf[k].astype(F32)
        drain(buf.at[pl.ds(0, count - 1)], send_sem)
        return total

    def flip_tile(c, carry):
        tiles_t[c] = tiles[c].T
        return carry

    sibling = (f, s, 1 - r)
    own_rows = pl.ds(r * SHARE, SHARE)
    hess_copy = remote(
        hess_t.at[own_rows], hess_t.at[own_rows], h_send.at[0], h_recv.at[0], sibling
    )
    thr_copy = remote(thr.at[r], thr.at[r], h_send.at[1], h_recv.at[1], sibling)

    def prepare_hess():
        for copy in later:
            copy.wait()

        def flip_hess(i, carry):
            block = hess[i]
            hess_t[r * SHARE + i] = block.T.astype(BF16)
            on_diag = iota((WIDTH, WIDTH), 0) == iota((WIDTH, WIDTH), 1)
            diagonal = jnp.sum(jnp.where(on_diag, block, 0.0), axis=0, keepdims=True)
            thr[r, pl.ds(i, 1), :] = penalty * diagonal
            return carry

        lax.fori_loop(0, SHARE, flip_hess, 0)
        hess_copy.start()
        thr_copy.start()
        sub = iota((OWNED, WIDTH), 0)

        def find(p, found):
            return found + jnp.where(order[0, p] == s * OWNED + sub, 1, 0)

        first = lax.fori_loop(
            0, BLOCKS // SEGMENTS, find, jnp.zeros((OWNED, WIDTH), jnp.int32), unroll=True
        )
        segment[...] = 1 - first
        most = jnp.zeros((OWNED, WIDTH), jnp.int32)
        for i in range(OWNED):
            most = jnp.where(sub == i, sweeps[s * OWNED + i], most)
        limit[...] = most

    def sum_rows(part, slot, between):
        xb, yb = x_buf.at[slot], y_buf.at[slot]
        xs, xr, ys, yr = x_send.at[slot], x_recv.at[slot], y_send.at[slot], y_recv.at[slot]
        line_start(xb, part.astype(BF16), me_x, NX, xs, xr, x_dev)
        between()
        total = line_finish(xb, NX, xs, xr)
        line_start(yb, total.astype(BF16), me_y, NY, ys, yr, y_dev)
        return line_finish(yb, NY, ys, yr)

    for copy in loads:
        copy.wait()

    for z in range(NZ):
        base = 2 * OWNED * z
        vecs[base : base + OWNED] = weights[pl.ds(base, OWNED, stride=2)]
        vecs[base + OWNED : base + 2 * OWNED] = weights[pl.ds(base + 1, OWNED, stride=2)]
    mine_at = pl.multiple_of(s * 2 * OWNED, 2 * OWNED)
    w_own[:, :HALF] = vecs[pl.ds(mine_at, OWNED)]
    w_own[:, HALF:] = vecs[pl.ds(mine_at + OWNED, OWNED)]
    direc[...] = jnp.zeros((OWNED, WIDTH), F32)
    change_out[...] = jnp.zeros((GROUPS, TILE_ROWS), F32)
    fill_forward()
    for k, copy in enumerate(pieces):
        copy.wait()
        lax.fori_loop(k * per_piece, (k + 1) * per_piece, flip_tile, 0, unroll=True)
    pl.semaphore_wait(barrier, NX + NY + NM - 3)

    def one_round(t, carry):
        def between():
            @pl.when(t == 0)
            def _():
                prepare_hess()

        summed = sum_rows(forward(), t % 2, between)

        @pl.when(t == 0)
        def _():
            prob = jax.nn.sigmoid(summed)
            curv[...] = prob * (1.0 - prob)
            rows[...] = prob - labels[...].astype(F32)

        @pl.when(t > 0)
        def _():
            change = change_out[...] + summed
            change_out[...] = change
            rows[...] = curv[...] * change

        contrib = backward()
        for z in range(NZ):
            block = contrib[OWNED * z : OWNED * (z + 1)]
            rs_out[z] = jnp.concatenate([block[:, :HALF], block[:, HALF:]], axis=0).astype(BF16)
        terms = rs_in.at[t % 2]
        for j in far_first(NM, NZ):
            dev = z_dev(j)
            send(rs_out.at[dev[1]], terms.at[me], z_send.at[0], z_recv.at[t % 2], dev)
        terms[me] = rs_out[s]
        drain(terms.at[pl.ds(0, NM - 1)], z_recv.at[t % 2])
        mine = terms[0].astype(F32)
        for k in range(1, NM):
            mine = mine + terms[k].astype(F32)
        mine = jnp.concatenate([mine[:OWNED], mine[OWNED:]], axis=1)
        drain(terms.at[pl.ds(0, NM - 1)], z_send.at[0])

        @pl.when(t == 0)
        def _():
            grad[...] = mine
            hess_copy.wait()
            thr_copy.wait()

        direction = direc[...]
        model_grad = grad[...] + jnp.where(t > 0, mine, 0.0) + ridge_term * direction
        high = model_grad.astype(BF16).astype(F32)
        pair = jnp.concatenate([high, model_grad - high], axis=0)
        at = iota((2 * OWNED, WIDTH), 0) % OWNED
        parts = [jnp.where(at == i, pair, 0.0).astype(BF16) for i in range(OWNED)]
        product = jnp.dot(
            jnp.concatenate(parts, axis=1),
            hess_t[...].reshape(OWNED * WIDTH, WIDTH),
            preferred_element_type=F32,
        )
        newton = product[:OWNED] + product[OWNED:]
        weight = w_own[...]
        trial = weight + direction - newton
        threshold = jnp.concatenate([thr[0], thr[1]], axis=0)
        size = jnp.maximum(jnp.abs(trial) - threshold, 0.0)
        shrunk = jnp.where(trial > 0.0, size, jnp.where(trial < 0.0, -size, 0.0))
        active = (segment[...] == t % SEGMENTS) & (t // SEGMENTS < limit[...])
        step = jnp.where(active, shrunk - weight - direction, 0.0)
        direc[...] = direction + step

        slot = ag_buf.at[s]
        slot[...] = jnp.concatenate([step[:, :HALF], step[:, HALF:]], axis=0).astype(BF16)
        for j in far_first(NZ, NZ):
            send(slot, slot, z_send.at[1], z_recv.at[2], z_same(j))
        drain(ag_buf.at[pl.ds(0, NZ - 1)], z_recv.at[2])
        vecs[...] = ag_buf[...].reshape(2 * BLOCKS, HALF).astype(F32)
        drain(ag_buf.at[pl.ds(0, NZ - 1)], z_send.at[1])
        fill_forward()
        return carry

    lax.fori_loop(0, ROUNDS, one_round, 0)

    direction = direc[...]
    weight = w_own[...]
    linear = grad[...] * direction + 0.5 * ridge_term * direction * direction
    linear = linear + penalty * (jnp.abs(weight + direction) - jnp.abs(weight))
    linear = jnp.where(iota((OWNED, WIDTH), 0) // SHARE == r, linear, 0.0)
    linear = linear[:, :HALF] + linear[:, HALF:]
    line_start(lx_buf, linear, me_x, NX, l_send.at[0], l_recv.at[0], x_dev)
    part = forward()
    linear = line_finish(lx_buf, NX, l_send.at[0], l_recv.at[0])
    line_start(ly_buf, linear, me_y, NY, l_send.at[1], l_recv.at[1], y_dev)
    summed = sum_rows(part, ROUNDS % 2, lambda: None)
    change = change_out[...] + summed
    linear = line_finish(ly_buf, NY, l_send.at[1], l_recv.at[1])
    quad = 0.5 * curv[...] * change * change
    for g in range(GROUPS // 8):
        linear = linear + quad[8 * g : 8 * g + 8]
    line_start(lz_buf, linear, me, NM, l_send.at[2], l_recv.at[2], z_dev)
    change_out[...] = change
    own = jnp.where(r == 0, direction[:SHARE], direction[SHARE:])
    dir_out[pl.ds(0, SHARE, stride=2)] = own[:, :HALF]
    dir_out[pl.ds(1, SHARE, stride=2)] = own[:, HALF:]
    total = line_finish(lz_buf, NM, l_send.at[2], l_recv.at[2])
    dec_out[...] = jnp.sum(jnp.sum(total, axis=0, keepdims=True), axis=1, keepdims=True)


def on_device(tiles, tile_block, tile_row, labels, weights, hess_inv, order, sweeps):
    vmem = pl.BlockSpec(memory_space=pltpu.VMEM)
    dma = pltpu.SemaphoreType.DMA
    direction, change, decrease = pl.pallas_call(
        body,
        out_shape=(
            jax.ShapeDtypeStruct((8, HALF), F32),
            jax.ShapeDtypeStruct((GROUPS, TILE_ROWS), F32),
            jax.ShapeDtypeStruct((1, 1), F32),
        ),
        in_specs=[pl.BlockSpec(memory_space=pltpu.HBM)] * 8,
        out_specs=[vmem] * 3,
        scratch_shapes=[
            pltpu.SMEM((1, 1, SLOTS), jnp.int32),
            pltpu.SMEM((1, 1, SLOTS), jnp.int32),
            pltpu.SMEM((1, BLOCKS), jnp.int32),
            pltpu.SMEM((BLOCKS,), jnp.int32),
            pltpu.VMEM((SLOTS, TILE_ROWS, WIDTH), BF16),
            pltpu.VMEM((GROUPS, TILE_ROWS), jnp.int32),
            pltpu.VMEM((2 * BLOCKS, HALF), F32),
            pltpu.VMEM((SHARE, WIDTH, WIDTH), F32),
            pltpu.VMEM((SLOTS, WIDTH, TILE_ROWS), BF16),
            pltpu.VMEM((OWNED, WIDTH, WIDTH), BF16),
            pltpu.VMEM((2 * BLOCKS, HALF), F32),
            pltpu.VMEM((GROUPS, TILE_ROWS), F32),
            pltpu.VMEM((GROUPS, SLOTS * WIDTH), BF16),
            pltpu.VMEM((BLOCKS, SLOTS * TILE_ROWS), BF16),
            pltpu.VMEM((2, SHARE, WIDTH), F32),
            pltpu.VMEM((OWNED, WIDTH), F32),
            pltpu.VMEM((OWNED, WIDTH), F32),
            pltpu.VMEM((OWNED, WIDTH), F32),
            pltpu.VMEM((OWNED, WIDTH), jnp.int32),
            pltpu.VMEM((OWNED, WIDTH), jnp.int32),
            pltpu.VMEM((GROUPS, TILE_ROWS), F32),
            pltpu.VMEM((2, NX, GROUPS, TILE_ROWS), BF16),
            pltpu.VMEM((2, NY, GROUPS, TILE_ROWS), BF16),
            pltpu.VMEM((NZ, 2 * OWNED, HALF), BF16),
            pltpu.VMEM((2, NM, 2 * OWNED, HALF), BF16),
            pltpu.VMEM((NZ, 2 * OWNED, HALF), BF16),
            pltpu.VMEM((NX, 8, HALF), F32),
            pltpu.VMEM((NY, 8, HALF), F32),
            pltpu.VMEM((NM, 8, HALF), F32),
            dma((2,)),
            dma((2,)),
            dma((2,)),
            dma((2,)),
            dma((2,)),
            dma((3,)),
            dma((3,)),
            dma((3,)),
            dma((2,)),
            dma((2,)),
            dma((7 + PIECES,)),
        ],
        compiler_params=pltpu.CompilerParams(
            collective_id=0, has_side_effects=True, vmem_limit_bytes=40 * 1024 * 1024
        ),
    )(
        tile_block,
        tile_row,
        order,
        sweeps,
        tiles.reshape(SLOTS, TILE_ROWS, WIDTH),
        labels.reshape(GROUPS, TILE_ROWS),
        weights.reshape(2 * BLOCKS, HALF),
        hess_inv,
    )
    return direction.reshape(-1), change.reshape(-1), decrease.reshape(1)


def solution(mesh):
    in_specs = (
        P("feat", ("samp", "rep"), None, None, None),
        P("feat", ("samp", "rep"), None),
        P("feat", ("samp", "rep"), None),
        P(("samp", "rep")),
        P("feat"),
        P(("feat", "samp", "rep"), None, None),
        P("feat", None),
        P("feat"),
    )
    out_specs = (P(("feat", "samp", "rep")), P(("samp", "rep")), P())
    return jax.shard_map(
        on_device, mesh=mesh, in_specs=in_specs, out_specs=out_specs, check_vma=False
    )
```

```python
import functools

import jax
import jax.numpy as jnp
from jax import lax
from jax.experimental import pallas as pl
from jax.experimental.pallas import tpu as pltpu
from jax.sharding import PartitionSpec as P

SWEEPS = 3
SEGMENTS = 2
ROUNDS = SWEEPS * SEGMENTS

NX = 4
NY = 8
NZ = 8
NM = 16
SLOTS = 32
TILE_ROWS = 128
WIDTH = 256
HALF = 128
GROUPS = 32
BLOCKS = 64
OWNED = 8
SHARE = 4
PIECES = 4

penalty = 0.05
ridge_term = 0.1

MESH = pl.DeviceIdType.MESH
F32 = jnp.float32
BF16 = jnp.bfloat16


def far_first(count, chips):
    per = count // chips
    return sorted(range(1, count), key=lambda j: -min(j // per, chips - j // per))


def iota(shape, dim):
    return lax.broadcasted_iota(jnp.int32, shape, dim)


def body(
    tile_block_hbm,
    tile_row_hbm,
    order_hbm,
    sweeps_hbm,
    tiles_hbm,
    labels_hbm,
    weights_hbm,
    hess_hbm,
    dir_out,
    change_out,
    dec_out,
    tile_block,
    tile_row,
    order,
    sweeps,
    tiles,
    labels,
    weights,
    hess,
    tiles_t,
    hess_t,
    vecs,
    rows,
    q_buf,
    p_buf,
    thr,
    w_own,
    grad,
    direc,
    segment,
    limit,
    curv,
    x_buf,
    y_buf,
    rs_out,
    rs_in,
    ag_buf,
    lx_buf,
    ly_buf,
    lz_buf,
    x_send,
    x_recv,
    y_send,
    y_recv,
    z_send,
    z_recv,
    l_send,
    l_recv,
    h_send,
    h_recv,
    load_sem,
):
    f, s, r = lax.axis_index("feat"), lax.axis_index("samp"), lax.axis_index("rep")
    me_x, me_y = f % NX, f // NX
    me = s * 2 + r

    def x_dev(j):
        return (me_y * NX + (me_x + j) % NX, s, r)

    def y_dev(j):
        return ((me_y + j) % NY * NX + me_x, s, r)

    def z_dev(j):
        return (f, (s + j // 2) % NZ, r ^ (j % 2))

    def z_same(j):
        return (f, (s + j) % NZ, r)

    barrier = pltpu.get_barrier_semaphore()
    for dev, count in ((y_dev, NY), (z_dev, NM), (x_dev, NX)):
        for j in far_first(count, min(count, 8)):
            pl.semaphore_signal(barrier, inc=1, device_id=dev(j), device_id_type=MESH)

    def load(src, dst, k):
        return pltpu.make_async_copy(src, dst, load_sem.at[k])

    loads = [
        load(tile_block_hbm, tile_block, 0),
        load(tile_row_hbm, tile_row, 1),
        load(weights_hbm, weights, 2),
    ]
    per_piece = SLOTS // PIECES
    pieces = [
        load(
            tiles_hbm.at[pl.ds(k * per_piece, per_piece)],
            tiles.at[pl.ds(k * per_piece, per_piece)],
            3 + k,
        )
        for k in range(PIECES)
    ]
    later = [
        load(hess_hbm, hess, 3 + PIECES),
        load(labels_hbm, labels, 4 + PIECES),
        load(order_hbm, order, 5 + PIECES),
        load(sweeps_hbm, sweeps, 6 + PIECES),
    ]
    for copy in loads + pieces + later:
        copy.start()

    row_iota = iota((GROUPS, HALF), 0)
    block_iota = iota((BLOCKS, TILE_ROWS), 0)

    def fill_forward():
        def fill(c, carry):
            b = tile_block[0, 0, c]
            live = b >= 0
            b = jnp.maximum(b, 0)
            at = 2 * OWNED * (b // OWNED) + b % OWNED
            group = jnp.where(live, tile_row[0, 0, c], -1)
            hot = row_iota == group
            left = jnp.where(hot, vecs[pl.ds(at, 1)], 0.0).astype(BF16)
            right = jnp.where(hot, vecs[pl.ds(at + OWNED, 1)], 0.0).astype(BF16)
            base = pl.multiple_of(c * WIDTH, WIDTH)
            q_buf[:, pl.ds(base, HALF)] = left
            q_buf[:, pl.ds(base + HALF, HALF)] = right
            return carry

        lax.fori_loop(0, SLOTS, fill, 0, unroll=True)

    def forward():
        flipped = tiles_t[...].reshape(SLOTS * WIDTH, TILE_ROWS)
        return jnp.dot(q_buf[...], flipped, preferred_element_type=F32)

    def backward():
        def fill(c, carry):
            b = tile_block[0, 0, c]
            picked = rows[pl.ds(tile_row[0, 0, c], 1)]
            base = pl.multiple_of(c * TILE_ROWS, TILE_ROWS)
            p_buf[:, pl.ds(base, TILE_ROWS)] = jnp.where(block_iota == b, picked, 0.0).astype(BF16)
            return carry

        lax.fori_loop(0, SLOTS, fill, 0, unroll=True)
        flat = tiles[...].reshape(SLOTS * TILE_ROWS, WIDTH)
        return jnp.dot(p_buf[...], flat, preferred_element_type=F32)

    def remote(src, dst, send_sem, recv_sem, dev):
        return pltpu.make_async_remote_copy(
            src_ref=src,
            dst_ref=dst,
            send_sem=send_sem,
            recv_sem=recv_sem,
            device_id=dev,
            device_id_type=MESH,
        )

    def send(src, dst, send_sem, recv_sem, dev):
        remote(src, dst, send_sem, recv_sem, dev).start()

    def drain(ref, sem):
        pltpu.make_async_copy(ref, ref, sem).wait()

    def line_start(buf, value, me_at, count, send_sem, recv_sem, dev):
        buf[me_at] = value
        for j in far_first(count, min(count, 8)):
            send(buf.at[me_at], buf.at[me_at], send_sem, recv_sem, dev(j))

    def line_finish(buf, count, send_sem, recv_sem):
        drain(buf.at[pl.ds(0, count - 1)], recv_sem)
        total = buf[0].astype(F32)
        for k in range(1, count):
            total = total + buf[k].astype(F32)
        drain(buf.at[pl.ds(0, count - 1)], send_sem)
        return total

    def flip_tile(c, carry):
        tiles_t[c] = tiles[c].T
        return carry

    sibling = (f, s, 1 - r)
    own_rows = pl.ds(r * SHARE, SHARE)
    hess_copy = remote(
        hess_t.at[own_rows], hess_t.at[own_rows], h_send.at[0], h_recv.at[0], sibling
    )
    thr_copy = remote(thr.at[r], thr.at[r], h_send.at[1], h_recv.at[1], sibling)

    def prepare_hess():
        for copy in later:
            copy.wait()

        def flip_hess(i, carry):
            block = hess[i]
            hess_t[r * SHARE + i] = block.T.astype(BF16)
            on_diag = iota((WIDTH, WIDTH), 0) == iota((WIDTH, WIDTH), 1)
            diagonal = jnp.sum(jnp.where(on_diag, block, 0.0), axis=0, keepdims=True)
            thr[r, pl.ds(i, 1), :] = penalty * diagonal
            return carry

        lax.fori_loop(0, SHARE, flip_hess, 0)
        hess_copy.start()
        thr_copy.start()
        sub = iota((OWNED, WIDTH), 0)

        def find(p, found):
            return found + jnp.where(order[0, p] == s * OWNED + sub, 1, 0)

        first = lax.fori_loop(
            0, BLOCKS // SEGMENTS, find, jnp.zeros((OWNED, WIDTH), jnp.int32), unroll=True
        )
        segment[...] = 1 - first
        most = jnp.zeros((OWNED, WIDTH), jnp.int32)
        for i in range(OWNED):
            most = jnp.where(sub == i, sweeps[s * OWNED + i], most)
        limit[...] = most

    def sum_rows(part, slot, between):
        xb, yb = x_buf.at[slot], y_buf.at[slot]
        xs, xr, ys, yr = x_send.at[slot], x_recv.at[slot], y_send.at[slot], y_recv.at[slot]
        line_start(xb, part.astype(BF16), me_x, NX, xs, xr, x_dev)
        between()
        total = line_finish(xb, NX, xs, xr)
        line_start(yb, total.astype(BF16), me_y, NY, ys, yr, y_dev)
        return line_finish(yb, NY, ys, yr)

    for copy in loads:
        copy.wait()

    for z in range(NZ):
        base = 2 * OWNED * z
        vecs[base : base + OWNED] = weights[pl.ds(base, OWNED, stride=2)]
        vecs[base + OWNED : base + 2 * OWNED] = weights[pl.ds(base + 1, OWNED, stride=2)]
    mine_at = pl.multiple_of(s * 2 * OWNED, 2 * OWNED)
    w_own[:, :HALF] = vecs[pl.ds(mine_at, OWNED)]
    w_own[:, HALF:] = vecs[pl.ds(mine_at + OWNED, OWNED)]
    direc[...] = jnp.zeros((OWNED, WIDTH), F32)
    change_out[...] = jnp.zeros((GROUPS, TILE_ROWS), F32)
    fill_forward()
    for k, copy in enumerate(pieces):
        copy.wait()
        lax.fori_loop(k * per_piece, (k + 1) * per_piece, flip_tile, 0, unroll=True)
    pl.semaphore_wait(barrier, NX + NY + NM - 3)

    def one_round(t, carry):
        def between():
            @pl.when(t == 0)
            def _():
                prepare_hess()

        summed = sum_rows(forward(), t % 2, between)

        @pl.when(t == 0)
        def _():
            prob = jax.nn.sigmoid(summed)
            curv[...] = prob * (1.0 - prob)
            rows[...] = prob - labels[...].astype(F32)

        @pl.when(t > 0)
        def _():
            change = change_out[...] + summed
            change_out[...] = change
            rows[...] = curv[...] * change

        contrib = backward()
        for z in range(NZ):
            block = contrib[OWNED * z : OWNED * (z + 1)]
            rs_out[z] = jnp.concatenate([block[:, :HALF], block[:, HALF:]], axis=0).astype(BF16)
        terms = rs_in.at[t % 2]
        for j in far_first(NM, NZ):
            dev = z_dev(j)
            send(rs_out.at[dev[1]], terms.at[me], z_send.at[0], z_recv.at[t % 2], dev)
        terms[me] = rs_out[s]
        drain(terms.at[pl.ds(0, NM - 1)], z_recv.at[t % 2])
        mine = terms[0].astype(F32)
        for k in range(1, NM):
            mine = mine + terms[k].astype(F32)
        mine = jnp.concatenate([mine[:OWNED], mine[OWNED:]], axis=1)
        drain(terms.at[pl.ds(0, NM - 1)], z_send.at[0])

        @pl.when(t == 0)
        def _():
            grad[...] = mine
            hess_copy.wait()
            thr_copy.wait()

        direction = direc[...]
        model_grad = grad[...] + jnp.where(t > 0, mine, 0.0) + ridge_term * direction
        high = model_grad.astype(BF16).astype(F32)
        pair = jnp.concatenate([high, model_grad - high], axis=0)
        at = iota((2 * OWNED, WIDTH), 0) % OWNED
        parts = [jnp.where(at == i, pair, 0.0).astype(BF16) for i in range(OWNED)]
        product = jnp.dot(
            jnp.concatenate(parts, axis=1),
            hess_t[...].reshape(OWNED * WIDTH, WIDTH),
            preferred_element_type=F32,
        )
        newton = product[:OWNED] + product[OWNED:]
        weight = w_own[...]
        trial = weight + direction - newton
        threshold = jnp.concatenate([thr[0], thr[1]], axis=0)
        size = jnp.maximum(jnp.abs(trial) - threshold, 0.0)
        shrunk = jnp.where(trial > 0.0, size, jnp.where(trial < 0.0, -size, 0.0))
        active = (segment[...] == t % SEGMENTS) & (t // SEGMENTS < limit[...])
        step = jnp.where(active, shrunk - weight - direction, 0.0)
        direc[...] = direction + step

        slot = ag_buf.at[s]
        slot[...] = jnp.concatenate([step[:, :HALF], step[:, HALF:]], axis=0).astype(BF16)
        for j in far_first(NZ, NZ):
            send(slot, slot, z_send.at[1], z_recv.at[2], z_same(j))
        drain(ag_buf.at[pl.ds(0, NZ - 1)], z_recv.at[2])
        vecs[...] = ag_buf[...].reshape(2 * BLOCKS, HALF).astype(F32)
        drain(ag_buf.at[pl.ds(0, NZ - 1)], z_send.at[1])
        fill_forward()
        return carry

    lax.fori_loop(0, ROUNDS, one_round, 0)

    direction = direc[...]
    weight = w_own[...]
    linear = grad[...] * direction + 0.5 * ridge_term * direction * direction
    linear = linear + penalty * (jnp.abs(weight + direction) - jnp.abs(weight))
    linear = jnp.where(iota((OWNED, WIDTH), 0) // SHARE == r, linear, 0.0)
    linear = linear[:, :HALF] + linear[:, HALF:]
    slot = ROUNDS % 2
    xb, yb = x_buf.at[slot], y_buf.at[slot]
    xs, xr, ys, yr = x_send.at[slot], x_recv.at[slot], y_send.at[slot], y_recv.at[slot]
    line_start(xb, forward().astype(BF16), me_x, NX, xs, xr, x_dev)
    line_start(lx_buf, linear, me_x, NX, l_send.at[0], l_recv.at[0], x_dev)
    total = line_finish(xb, NX, xs, xr)
    line_start(yb, total.astype(BF16), me_y, NY, ys, yr, y_dev)
    linear = line_finish(lx_buf, NX, l_send.at[0], l_recv.at[0])
    line_start(ly_buf, linear, me_y, NY, l_send.at[1], l_recv.at[1], y_dev)
    change = change_out[...] + line_finish(yb, NY, ys, yr)
    linear = line_finish(ly_buf, NY, l_send.at[1], l_recv.at[1])
    quad = 0.5 * curv[...] * change * change
    for g in range(GROUPS // 8):
        linear = linear + quad[8 * g : 8 * g + 8]
    line_start(lz_buf, linear, me, NM, l_send.at[2], l_recv.at[2], z_dev)
    change_out[...] = change
    own = jnp.where(r == 0, direction[:SHARE], direction[SHARE:])
    dir_out[pl.ds(0, SHARE, stride=2)] = own[:, :HALF]
    dir_out[pl.ds(1, SHARE, stride=2)] = own[:, HALF:]
    total = line_finish(lz_buf, NM, l_send.at[2], l_recv.at[2])
    dec_out[...] = jnp.sum(jnp.sum(total, axis=0, keepdims=True), axis=1, keepdims=True)


def on_device(tiles, tile_block, tile_row, labels, weights, hess_inv, order, sweeps):
    vmem = pl.BlockSpec(memory_space=pltpu.VMEM)
    dma = pltpu.SemaphoreType.DMA
    direction, change, decrease = pl.pallas_call(
        body,
        out_shape=(
            jax.ShapeDtypeStruct((8, HALF), F32),
            jax.ShapeDtypeStruct((GROUPS, TILE_ROWS), F32),
            jax.ShapeDtypeStruct((1, 1), F32),
        ),
        in_specs=[pl.BlockSpec(memory_space=pltpu.HBM)] * 8,
        out_specs=[vmem] * 3,
        scratch_shapes=[
            pltpu.SMEM((1, 1, SLOTS), jnp.int32),
            pltpu.SMEM((1, 1, SLOTS), jnp.int32),
            pltpu.SMEM((1, BLOCKS), jnp.int32),
            pltpu.SMEM((BLOCKS,), jnp.int32),
            pltpu.VMEM((SLOTS, TILE_ROWS, WIDTH), BF16),
            pltpu.VMEM((GROUPS, TILE_ROWS), jnp.int32),
            pltpu.VMEM((2 * BLOCKS, HALF), F32),
            pltpu.VMEM((SHARE, WIDTH, WIDTH), F32),
            pltpu.VMEM((SLOTS, WIDTH, TILE_ROWS), BF16),
            pltpu.VMEM((OWNED, WIDTH, WIDTH), BF16),
            pltpu.VMEM((2 * BLOCKS, HALF), F32),
            pltpu.VMEM((GROUPS, TILE_ROWS), F32),
            pltpu.VMEM((GROUPS, SLOTS * WIDTH), BF16),
            pltpu.VMEM((BLOCKS, SLOTS * TILE_ROWS), BF16),
            pltpu.VMEM((2, SHARE, WIDTH), F32),
            pltpu.VMEM((OWNED, WIDTH), F32),
            pltpu.VMEM((OWNED, WIDTH), F32),
            pltpu.VMEM((OWNED, WIDTH), F32),
            pltpu.VMEM((OWNED, WIDTH), jnp.int32),
            pltpu.VMEM((OWNED, WIDTH), jnp.int32),
            pltpu.VMEM((GROUPS, TILE_ROWS), F32),
            pltpu.VMEM((2, NX, GROUPS, TILE_ROWS), BF16),
            pltpu.VMEM((2, NY, GROUPS, TILE_ROWS), BF16),
            pltpu.VMEM((NZ, 2 * OWNED, HALF), BF16),
            pltpu.VMEM((2, NM, 2 * OWNED, HALF), BF16),
            pltpu.VMEM((NZ, 2 * OWNED, HALF), BF16),
            pltpu.VMEM((NX, 8, HALF), F32),
            pltpu.VMEM((NY, 8, HALF), F32),
            pltpu.VMEM((NM, 8, HALF), F32),
            dma((2,)),
            dma((2,)),
            dma((2,)),
            dma((2,)),
            dma((2,)),
            dma((3,)),
            dma((3,)),
            dma((3,)),
            dma((2,)),
            dma((2,)),
            dma((7 + PIECES,)),
        ],
        compiler_params=pltpu.CompilerParams(
            collective_id=0, has_side_effects=True, vmem_limit_bytes=60 * 1024 * 1024
        ),
    )(
        tile_block,
        tile_row,
        order,
        sweeps,
        tiles.reshape(SLOTS, TILE_ROWS, WIDTH),
        labels.reshape(GROUPS, TILE_ROWS),
        weights.reshape(2 * BLOCKS, HALF),
        hess_inv,
    )
    return direction.reshape(-1), change.reshape(-1), decrease.reshape(1)


def solution(mesh):
    in_specs = (
        P("feat", ("samp", "rep"), None, None, None),
        P("feat", ("samp", "rep"), None),
        P("feat", ("samp", "rep"), None),
        P(("samp", "rep")),
        P("feat"),
        P(("feat", "samp", "rep"), None, None),
        P("feat", None),
        P("feat"),
    )
    out_specs = (P(("feat", "samp", "rep")), P(("samp", "rep")), P())
    return jax.shard_map(
        on_device, mesh=mesh, in_specs=in_specs, out_specs=out_specs, check_vma=False
    )
```

```python
import functools

import jax
import jax.numpy as jnp
from jax import lax
from jax.experimental import pallas as pl
from jax.experimental.pallas import tpu as pltpu
from jax.sharding import PartitionSpec as P

SWEEPS = 3
SEGMENTS = 2
ROUNDS = SWEEPS * SEGMENTS

NX = 4
NY = 8
NZ = 8
NM = 16
SLOTS = 32
TILE_ROWS = 128
WIDTH = 256
HALF = 128
GROUPS = 32
BLOCKS = 64
OWNED = 8
SHARE = 4
PIECES = 4

penalty = 0.05
ridge_term = 0.1

MESH = pl.DeviceIdType.MESH
F32 = jnp.float32
BF16 = jnp.bfloat16


def far_first(count, chips):
    per = count // chips
    return sorted(range(1, count), key=lambda j: (-min(j // per, chips - j // per), -(j % per)))


def iota(shape, dim):
    return lax.broadcasted_iota(jnp.int32, shape, dim)


def body(
    tile_block_hbm,
    tile_row_hbm,
    order_hbm,
    sweeps_hbm,
    tiles_hbm,
    labels_hbm,
    weights_hbm,
    hess_hbm,
    dir_out,
    change_out,
    dec_out,
    tile_block,
    tile_row,
    order,
    sweeps,
    tiles,
    labels,
    weights,
    hess,
    tiles_t,
    hess_t,
    vecs,
    rows,
    q_buf,
    p_buf,
    thr,
    w_own,
    grad,
    direc,
    segment,
    limit,
    curv,
    x_buf,
    y_buf,
    rs_out,
    rs_in,
    ag_buf,
    lx_buf,
    ly_buf,
    lz_buf,
    x_send,
    x_recv,
    y_send,
    y_recv,
    z_send,
    z_recv,
    l_send,
    l_recv,
    h_send,
    h_recv,
    load_sem,
):
    f, s, r = lax.axis_index("feat"), lax.axis_index("samp"), lax.axis_index("rep")
    me_x, me_y = f % NX, f // NX
    me = s * 2 + r

    def x_dev(j):
        return (me_y * NX + (me_x + j) % NX, s, r)

    def y_dev(j):
        return ((me_y + j) % NY * NX + me_x, s, r)

    def z_dev(j):
        return (f, (s + j // 2) % NZ, r ^ (j % 2))

    def z_same(j):
        return (f, (s + j) % NZ, r)

    barrier = pltpu.get_barrier_semaphore()
    for dev, count in ((y_dev, NY), (z_dev, NM), (x_dev, NX)):
        for j in far_first(count, min(count, 8)):
            pl.semaphore_signal(barrier, inc=1, device_id=dev(j), device_id_type=MESH)

    def load(src, dst, k):
        return pltpu.make_async_copy(src, dst, load_sem.at[k])

    loads = [
        load(tile_block_hbm, tile_block, 0),
        load(tile_row_hbm, tile_row, 1),
        load(weights_hbm, weights, 2),
    ]
    per_piece = SLOTS // PIECES
    pieces = [
        load(
            tiles_hbm.at[pl.ds(k * per_piece, per_piece)],
            tiles.at[pl.ds(k * per_piece, per_piece)],
            3 + k,
        )
        for k in range(PIECES)
    ]
    later = [
        load(hess_hbm, hess, 3 + PIECES),
        load(labels_hbm, labels, 4 + PIECES),
        load(order_hbm, order, 5 + PIECES),
        load(sweeps_hbm, sweeps, 6 + PIECES),
    ]
    for copy in loads + pieces + later:
        copy.start()

    row_iota = iota((GROUPS, HALF), 0)
    block_iota = iota((BLOCKS, TILE_ROWS), 0)

    def fill_forward():
        def fill(c, carry):
            b = tile_block[0, 0, c]
            live = b >= 0
            b = jnp.maximum(b, 0)
            at = 2 * OWNED * (b // OWNED) + b % OWNED
            group = jnp.where(live, tile_row[0, 0, c], -1)
            hot = row_iota == group
            left = jnp.where(hot, vecs[pl.ds(at, 1)], 0.0).astype(BF16)
            right = jnp.where(hot, vecs[pl.ds(at + OWNED, 1)], 0.0).astype(BF16)
            base = pl.multiple_of(c * WIDTH, WIDTH)
            q_buf[:, pl.ds(base, HALF)] = left
            q_buf[:, pl.ds(base + HALF, HALF)] = right
            return carry

        lax.fori_loop(0, SLOTS, fill, 0, unroll=True)

    def forward():
        flipped = tiles_t[...].reshape(SLOTS * WIDTH, TILE_ROWS)
        return jnp.dot(q_buf[...], flipped, preferred_element_type=F32)

    def backward():
        def fill(c, carry):
            b = tile_block[0, 0, c]
            picked = rows[pl.ds(tile_row[0, 0, c], 1)]
            base = pl.multiple_of(c * TILE_ROWS, TILE_ROWS)
            p_buf[:, pl.ds(base, TILE_ROWS)] = jnp.where(block_iota == b, picked, 0.0).astype(BF16)
            return carry

        lax.fori_loop(0, SLOTS, fill, 0, unroll=True)
        flat = tiles[...].reshape(SLOTS * TILE_ROWS, WIDTH)
        left = jnp.dot(p_buf[...], flat[:, :HALF], preferred_element_type=F32)
        right = jnp.dot(p_buf[...], flat[:, HALF:], preferred_element_type=F32)
        return left, right

    def remote(src, dst, send_sem, recv_sem, dev):
        return pltpu.make_async_remote_copy(
            src_ref=src,
            dst_ref=dst,
            send_sem=send_sem,
            recv_sem=recv_sem,
            device_id=dev,
            device_id_type=MESH,
        )

    def send(src, dst, send_sem, recv_sem, dev):
        remote(src, dst, send_sem, recv_sem, dev).start()

    def drain(ref, sem):
        pltpu.make_async_copy(ref, ref, sem).wait()

    def line_start(buf, value, me_at, count, send_sem, recv_sem, dev):
        buf[me_at] = value
        for j in far_first(count, min(count, 8)):
            send(buf.at[me_at], buf.at[me_at], send_sem, recv_sem, dev(j))

    def line_finish(buf, count, send_sem, recv_sem):
        drain(buf.at[pl.ds(0, count - 1)], recv_sem)
        total = buf[0].astype(F32)
        for k in range(1, count):
            total = total + buf[k].astype(F32)
        drain(buf.at[pl.ds(0, count - 1)], send_sem)
        return total

    def flip_tile(c, carry):
        tiles_t[c] = tiles[c].T
        return carry

    sibling = (f, s, 1 - r)
    own_rows = pl.ds(r * SHARE, SHARE)
    hess_copy = remote(
        hess_t.at[own_rows], hess_t.at[own_rows], h_send.at[0], h_recv.at[0], sibling
    )
    thr_copy = remote(thr.at[r], thr.at[r], h_send.at[1], h_recv.at[1], sibling)

    def prepare_hess():
        for copy in later:
            copy.wait()

        def flip_hess(i, carry):
            block = hess[i]
            hess_t[r * SHARE + i] = block.T.astype(BF16)
            on_diag = iota((WIDTH, WIDTH), 0) == iota((WIDTH, WIDTH), 1)
            diagonal = jnp.sum(jnp.where(on_diag, block, 0.0), axis=0, keepdims=True)
            thr[r, pl.ds(i, 1), :] = penalty * diagonal
            return carry

        lax.fori_loop(0, SHARE, flip_hess, 0)
        hess_copy.start()
        thr_copy.start()
        sub = iota((OWNED, WIDTH), 0)

        def find(p, found):
            return found + jnp.where(order[0, p] == s * OWNED + sub, 1, 0)

        first = lax.fori_loop(
            0, BLOCKS // SEGMENTS, find, jnp.zeros((OWNED, WIDTH), jnp.int32), unroll=True
        )
        segment[...] = 1 - first
        most = jnp.zeros((OWNED, WIDTH), jnp.int32)
        for i in range(OWNED):
            most = jnp.where(sub == i, sweeps[s * OWNED + i], most)
        limit[...] = most

    def sum_rows(part, slot, between):
        xb, yb = x_buf.at[slot], y_buf.at[slot]
        xs, xr, ys, yr = x_send.at[slot], x_recv.at[slot], y_send.at[slot], y_recv.at[slot]
        line_start(xb, part.astype(BF16), me_x, NX, xs, xr, x_dev)
        between()
        total = line_finish(xb, NX, xs, xr)
        line_start(yb, total.astype(BF16), me_y, NY, ys, yr, y_dev)
        return line_finish(yb, NY, ys, yr)

    for copy in loads:
        copy.wait()

    for z in range(NZ):
        base = 2 * OWNED * z
        vecs[base : base + OWNED] = weights[pl.ds(base, OWNED, stride=2)]
        vecs[base + OWNED : base + 2 * OWNED] = weights[pl.ds(base + 1, OWNED, stride=2)]
    mine_at = pl.multiple_of(s * 2 * OWNED, 2 * OWNED)
    w_own[:, :HALF] = vecs[pl.ds(mine_at, OWNED)]
    w_own[:, HALF:] = vecs[pl.ds(mine_at + OWNED, OWNED)]
    direc[...] = jnp.zeros((OWNED, WIDTH), F32)
    change_out[...] = jnp.zeros((GROUPS, TILE_ROWS), F32)
    fill_forward()
    for k, copy in enumerate(pieces):
        copy.wait()
        lax.fori_loop(k * per_piece, (k + 1) * per_piece, flip_tile, 0, unroll=True)
    pl.semaphore_wait(barrier, NX + NY + NM - 3)

    def one_round(t, carry):
        def between():
            @pl.when(t == 0)
            def _():
                prepare_hess()

        summed = sum_rows(forward(), t % 2, between)

        @pl.when(t == 0)
        def _():
            prob = jax.nn.sigmoid(summed)
            curv[...] = prob * (1.0 - prob)
            rows[...] = prob - labels[...].astype(F32)

        @pl.when(t > 0)
        def _():
            change = change_out[...] + summed
            change_out[...] = change
            rows[...] = curv[...] * change

        left, right = backward()
        for z in range(NZ):
            at = slice(OWNED * z, OWNED * (z + 1))
            rs_out[z] = jnp.concatenate([left[at], right[at]], axis=0).astype(BF16)
        terms = rs_in.at[t % 2]
        for j in far_first(NM, NZ):
            dev = z_dev(j)
            send(rs_out.at[dev[1]], terms.at[me], z_send.at[0], z_recv.at[t % 2], dev)
        terms[me] = rs_out[s]
        drain(terms.at[pl.ds(0, NM - 1)], z_recv.at[t % 2])
        mine = terms[0].astype(F32)
        for k in range(1, NM):
            mine = mine + terms[k].astype(F32)
        mine = jnp.concatenate([mine[:OWNED], mine[OWNED:]], axis=1)
        drain(terms.at[pl.ds(0, NM - 1)], z_send.at[0])

        @pl.when(t == 0)
        def _():
            grad[...] = mine
            hess_copy.wait()
            thr_copy.wait()

        direction = direc[...]
        model_grad = grad[...] + jnp.where(t > 0, mine, 0.0) + ridge_term * direction
        high = model_grad.astype(BF16).astype(F32)
        pair = jnp.concatenate([high, model_grad - high], axis=0)
        at = iota((2 * OWNED, WIDTH), 0) % OWNED
        parts = [jnp.where(at == i, pair, 0.0).astype(BF16) for i in range(OWNED)]
        product = jnp.dot(
            jnp.concatenate(parts, axis=1),
            hess_t[...].reshape(OWNED * WIDTH, WIDTH),
            preferred_element_type=F32,
        )
        newton = product[:OWNED] + product[OWNED:]
        weight = w_own[...]
        trial = weight + direction - newton
        threshold = jnp.concatenate([thr[0], thr[1]], axis=0)
        size = jnp.maximum(jnp.abs(trial) - threshold, 0.0)
        shrunk = jnp.where(trial > 0.0, size, jnp.where(trial < 0.0, -size, 0.0))
        active = (segment[...] == t % SEGMENTS) & (t // SEGMENTS < limit[...])
        step = jnp.where(active, shrunk - weight - direction, 0.0)
        direc[...] = direction + step

        slot = ag_buf.at[s]
        slot[...] = jnp.concatenate([step[:, :HALF], step[:, HALF:]], axis=0).astype(BF16)
        for j in far_first(NZ, NZ):
            send(slot, slot, z_send.at[1], z_recv.at[2], z_same(j))
        drain(ag_buf.at[pl.ds(0, NZ - 1)], z_recv.at[2])
        vecs[...] = ag_buf[...].reshape(2 * BLOCKS, HALF).astype(F32)
        drain(ag_buf.at[pl.ds(0, NZ - 1)], z_send.at[1])
        fill_forward()
        return carry

    lax.fori_loop(0, ROUNDS, one_round, 0)

    direction = direc[...]
    weight = w_own[...]
    linear = grad[...] * direction + 0.5 * ridge_term * direction * direction
    linear = linear + penalty * (jnp.abs(weight + direction) - jnp.abs(weight))
    linear = jnp.where(iota((OWNED, WIDTH), 0) // SHARE == r, linear, 0.0)
    linear = linear[:, :HALF] + linear[:, HALF:]
    slot = ROUNDS % 2
    xb, yb = x_buf.at[slot], y_buf.at[slot]
    xs, xr, ys, yr = x_send.at[slot], x_recv.at[slot], y_send.at[slot], y_recv.at[slot]
    line_start(xb, forward().astype(BF16), me_x, NX, xs, xr, x_dev)
    line_start(lx_buf, linear, me_x, NX, l_send.at[0], l_recv.at[0], x_dev)
    total = line_finish(xb, NX, xs, xr)
    line_start(yb, total.astype(BF16), me_y, NY, ys, yr, y_dev)
    linear = line_finish(lx_buf, NX, l_send.at[0], l_recv.at[0])
    line_start(ly_buf, linear, me_y, NY, l_send.at[1], l_recv.at[1], y_dev)
    change = change_out[...] + line_finish(yb, NY, ys, yr)
    linear = line_finish(ly_buf, NY, l_send.at[1], l_recv.at[1])
    quad = 0.5 * curv[...] * change * change
    for g in range(GROUPS // 8):
        linear = linear + quad[8 * g : 8 * g + 8]
    line_start(lz_buf, linear, me, NM, l_send.at[2], l_recv.at[2], z_dev)
    change_out[...] = change
    own = jnp.where(r == 0, direction[:SHARE], direction[SHARE:])
    dir_out[pl.ds(0, SHARE, stride=2)] = own[:, :HALF]
    dir_out[pl.ds(1, SHARE, stride=2)] = own[:, HALF:]
    total = line_finish(lz_buf, NM, l_send.at[2], l_recv.at[2])
    dec_out[...] = jnp.sum(jnp.sum(total, axis=0, keepdims=True), axis=1, keepdims=True)


def write_out(direction, change, dir_out, change_out, sem):
    first = pltpu.make_async_copy(direction, dir_out, sem.at[0])
    second = pltpu.make_async_copy(change, change_out, sem.at[1])
    first.start()
    second.start()
    first.wait()
    second.wait()


def on_device(tiles, tile_block, tile_row, labels, weights, hess_inv, order, sweeps):
    vmem = pl.BlockSpec(memory_space=pltpu.VMEM)
    hbm = pl.BlockSpec(memory_space=pltpu.HBM)
    dma = pltpu.SemaphoreType.DMA
    direction, change, decrease = pl.pallas_call(
        body,
        out_shape=(
            jax.ShapeDtypeStruct((8, HALF), F32),
            jax.ShapeDtypeStruct((GROUPS, TILE_ROWS), F32),
            jax.ShapeDtypeStruct((1, 1), F32),
        ),
        in_specs=[hbm] * 8,
        out_specs=[vmem] * 3,
        scratch_shapes=[
            pltpu.SMEM((1, 1, SLOTS), jnp.int32),
            pltpu.SMEM((1, 1, SLOTS), jnp.int32),
            pltpu.SMEM((1, BLOCKS), jnp.int32),
            pltpu.SMEM((BLOCKS,), jnp.int32),
            pltpu.VMEM((SLOTS, TILE_ROWS, WIDTH), BF16),
            pltpu.VMEM((GROUPS, TILE_ROWS), jnp.int32),
            pltpu.VMEM((2 * BLOCKS, HALF), F32),
            pltpu.VMEM((SHARE, WIDTH, WIDTH), F32),
            pltpu.VMEM((SLOTS, WIDTH, TILE_ROWS), BF16),
            pltpu.VMEM((OWNED, WIDTH, WIDTH), BF16),
            pltpu.VMEM((2 * BLOCKS, HALF), F32),
            pltpu.VMEM((GROUPS, TILE_ROWS), F32),
            pltpu.VMEM((GROUPS, SLOTS * WIDTH), BF16),
            pltpu.VMEM((BLOCKS, SLOTS * TILE_ROWS), BF16),
            pltpu.VMEM((2, SHARE, WIDTH), F32),
            pltpu.VMEM((OWNED, WIDTH), F32),
            pltpu.VMEM((OWNED, WIDTH), F32),
            pltpu.VMEM((OWNED, WIDTH), F32),
            pltpu.VMEM((OWNED, WIDTH), jnp.int32),
            pltpu.VMEM((OWNED, WIDTH), jnp.int32),
            pltpu.VMEM((GROUPS, TILE_ROWS), F32),
            pltpu.VMEM((2, NX, GROUPS, TILE_ROWS), BF16),
            pltpu.VMEM((2, NY, GROUPS, TILE_ROWS), BF16),
            pltpu.VMEM((NZ, 2 * OWNED, HALF), BF16),
            pltpu.VMEM((2, NM, 2 * OWNED, HALF), BF16),
            pltpu.VMEM((NZ, 2 * OWNED, HALF), BF16),
            pltpu.VMEM((NX, 8, HALF), F32),
            pltpu.VMEM((NY, 8, HALF), F32),
            pltpu.VMEM((NM, 8, HALF), F32),
            dma((2,)),
            dma((2,)),
            dma((2,)),
            dma((2,)),
            dma((2,)),
            dma((3,)),
            dma((3,)),
            dma((3,)),
            dma((2,)),
            dma((2,)),
            dma((7 + PIECES,)),
        ],
        compiler_params=pltpu.CompilerParams(
            collective_id=0, has_side_effects=True, vmem_limit_bytes=60 * 1024 * 1024
        ),
    )(
        tile_block,
        tile_row,
        order,
        sweeps,
        tiles.reshape(SLOTS, TILE_ROWS, WIDTH),
        labels.reshape(GROUPS, TILE_ROWS),
        weights.reshape(2 * BLOCKS, HALF),
        hess_inv,
    )
    direction, change = pl.pallas_call(
        write_out,
        out_shape=(
            jax.ShapeDtypeStruct((8, HALF), F32),
            jax.ShapeDtypeStruct((GROUPS, TILE_ROWS), F32),
        ),
        in_specs=[hbm] * 2,
        out_specs=[hbm] * 2,
        scratch_shapes=[dma((2,))],
        compiler_params=pltpu.CompilerParams(vmem_limit_bytes=60 * 1024 * 1024),
    )(direction, change)
    return direction.reshape(-1), change.reshape(-1), decrease.reshape(1)


def solution(mesh):
    in_specs = (
        P("feat", ("samp", "rep"), None, None, None),
        P("feat", ("samp", "rep"), None),
        P("feat", ("samp", "rep"), None),
        P(("samp", "rep")),
        P("feat"),
        P(("feat", "samp", "rep"), None, None),
        P("feat", None),
        P("feat"),
    )
    out_specs = (P(("feat", "samp", "rep")), P(("samp", "rep")), P())
    return jax.shard_map(
        on_device, mesh=mesh, in_specs=in_specs, out_specs=out_specs, check_vma=False
    )
```

```python
import functools

import jax
import jax.numpy as jnp
from jax import lax
from jax.experimental import pallas as pl
from jax.experimental.pallas import tpu as pltpu
from jax.sharding import PartitionSpec as P

SWEEPS = 3
SEGMENTS = 2
ROUNDS = SWEEPS * SEGMENTS

NX = 4
NY = 8
NZ = 8
NM = 16
SLOTS = 32
TILE_ROWS = 128
WIDTH = 256
HALF = 128
GROUPS = 32
BLOCKS = 64
OWNED = 8
SHARE = 4
PIECES = 4

penalty = 0.05
ridge_term = 0.1

MESH = pl.DeviceIdType.MESH
F32 = jnp.float32
BF16 = jnp.bfloat16


def far_first(count, chips):
    per = count // chips
    return sorted(range(1, count), key=lambda j: (-min(j // per, chips - j // per), -(j % per)))


def iota(shape, dim):
    return lax.broadcasted_iota(jnp.int32, shape, dim)


def body(
    tile_block_hbm,
    tile_row_hbm,
    order_hbm,
    sweeps_hbm,
    tiles_hbm,
    labels_hbm,
    weights_hbm,
    hess_hbm,
    dir_out,
    change_out,
    dec_out,
    tile_block,
    tile_row,
    order,
    sweeps,
    tiles,
    labels,
    weights,
    hess,
    tiles_t,
    hess_t,
    vecs,
    rows,
    q_buf,
    p_buf,
    thr,
    w_own,
    grad,
    direc,
    segment,
    limit,
    curv,
    x_buf,
    y_buf,
    rs_out,
    rs_in,
    ag_buf,
    lx_buf,
    ly_buf,
    lz_buf,
    x_send,
    x_recv,
    y_send,
    y_recv,
    z_send,
    z_recv,
    l_send,
    l_recv,
    h_send,
    h_recv,
    load_sem,
):
    f, s, r = lax.axis_index("feat"), lax.axis_index("samp"), lax.axis_index("rep")
    me_x, me_y = f % NX, f // NX
    me = s * 2 + r

    def x_dev(j):
        return (me_y * NX + (me_x + j) % NX, s, r)

    def y_dev(j):
        return ((me_y + j) % NY * NX + me_x, s, r)

    def z_dev(j):
        return (f, (s + j // 2) % NZ, r ^ (j % 2))

    def z_same(j):
        return (f, (s + j) % NZ, r)

    barrier = pltpu.get_barrier_semaphore()
    for dev, count in ((y_dev, NY), (z_dev, NM), (x_dev, NX)):
        for j in far_first(count, min(count, 8)):
            pl.semaphore_signal(barrier, inc=1, device_id=dev(j), device_id_type=MESH)

    def load(src, dst, k):
        return pltpu.make_async_copy(src, dst, load_sem.at[k])

    loads = [
        load(tile_block_hbm, tile_block, 0),
        load(tile_row_hbm, tile_row, 1),
        load(weights_hbm, weights, 2),
    ]
    per_piece = SLOTS // PIECES
    pieces = [
        load(
            tiles_hbm.at[pl.ds(k * per_piece, per_piece)],
            tiles.at[pl.ds(k * per_piece, per_piece)],
            3 + k,
        )
        for k in range(PIECES)
    ]
    later = [
        load(hess_hbm, hess, 3 + PIECES),
        load(labels_hbm, labels, 4 + PIECES),
        load(order_hbm, order, 5 + PIECES),
        load(sweeps_hbm, sweeps, 6 + PIECES),
    ]
    for copy in loads + pieces + later:
        copy.start()

    row_iota = iota((GROUPS, HALF), 0)
    block_iota = iota((BLOCKS, TILE_ROWS), 0)

    def fill_forward():
        def fill(c, carry):
            b = tile_block[0, 0, c]
            live = b >= 0
            b = jnp.maximum(b, 0)
            at = 2 * OWNED * (b // OWNED) + b % OWNED
            group = jnp.where(live, tile_row[0, 0, c], -1)
            hot = row_iota == group
            left = jnp.where(hot, vecs[pl.ds(at, 1)], 0.0).astype(BF16)
            right = jnp.where(hot, vecs[pl.ds(at + OWNED, 1)], 0.0).astype(BF16)
            base = pl.multiple_of(c * WIDTH, WIDTH)
            q_buf[:, pl.ds(base, HALF)] = left
            q_buf[:, pl.ds(base + HALF, HALF)] = right
            return carry

        lax.fori_loop(0, SLOTS, fill, 0, unroll=True)

    def forward():
        flipped = tiles_t[...].reshape(SLOTS * WIDTH, TILE_ROWS)
        return jnp.dot(q_buf[...], flipped, preferred_element_type=F32)

    def backward():
        def fill(c, carry):
            b = tile_block[0, 0, c]
            picked = rows[pl.ds(tile_row[0, 0, c], 1)]
            base = pl.multiple_of(c * TILE_ROWS, TILE_ROWS)
            p_buf[:, pl.ds(base, TILE_ROWS)] = jnp.where(block_iota == b, picked, 0.0).astype(BF16)
            return carry

        lax.fori_loop(0, SLOTS, fill, 0, unroll=True)
        flat = tiles[...].reshape(SLOTS * TILE_ROWS, WIDTH)
        left = jnp.dot(p_buf[...], flat[:, :HALF], preferred_element_type=F32)
        right = jnp.dot(p_buf[...], flat[:, HALF:], preferred_element_type=F32)
        return left, right

    def remote(src, dst, send_sem, recv_sem, dev):
        return pltpu.make_async_remote_copy(
            src_ref=src,
            dst_ref=dst,
            send_sem=send_sem,
            recv_sem=recv_sem,
            device_id=dev,
            device_id_type=MESH,
        )

    def send(src, dst, send_sem, recv_sem, dev):
        remote(src, dst, send_sem, recv_sem, dev).start()

    def drain(ref, sem):
        pltpu.make_async_copy(ref, ref, sem).wait()

    def line_start(buf, value, me_at, count, send_sem, recv_sem, dev):
        buf[me_at] = value
        for j in far_first(count, min(count, 8)):
            send(buf.at[me_at], buf.at[me_at], send_sem, recv_sem, dev(j))

    def line_finish(buf, count, send_sem, recv_sem):
        drain(buf.at[pl.ds(0, count - 1)], recv_sem)
        total = buf[0].astype(F32)
        for k in range(1, count):
            total = total + buf[k].astype(F32)
        drain(buf.at[pl.ds(0, count - 1)], send_sem)
        return total

    def flip_tile(c, carry):
        tiles_t[c] = tiles[c].T
        return carry

    sibling = (f, s, 1 - r)
    own_rows = pl.ds(r * SHARE, SHARE)
    hess_copy = remote(
        hess_t.at[own_rows], hess_t.at[own_rows], h_send.at[0], h_recv.at[0], sibling
    )
    thr_copy = remote(thr.at[r], thr.at[r], h_send.at[1], h_recv.at[1], sibling)

    def prepare_hess():
        for copy in later:
            copy.wait()

        def flip_hess(i, carry):
            block = hess[i]
            hess_t[r * SHARE + i] = block.T.astype(BF16)
            on_diag = iota((WIDTH, WIDTH), 0) == iota((WIDTH, WIDTH), 1)
            diagonal = jnp.sum(jnp.where(on_diag, block, 0.0), axis=0, keepdims=True)
            thr[r, pl.ds(i, 1), :] = penalty * diagonal
            return carry

        lax.fori_loop(0, SHARE, flip_hess, 0)
        hess_copy.start()
        thr_copy.start()
        sub = iota((OWNED, WIDTH), 0)

        def find(p, found):
            return found + jnp.where(order[0, p] == s * OWNED + sub, 1, 0)

        first = lax.fori_loop(
            0, BLOCKS // SEGMENTS, find, jnp.zeros((OWNED, WIDTH), jnp.int32), unroll=True
        )
        segment[...] = 1 - first
        most = jnp.zeros((OWNED, WIDTH), jnp.int32)
        for i in range(OWNED):
            most = jnp.where(sub == i, sweeps[s * OWNED + i], most)
        limit[...] = most

    def sum_rows(part, slot, between):
        xb, yb = x_buf.at[slot], y_buf.at[slot]
        xs, xr, ys, yr = x_send.at[slot], x_recv.at[slot], y_send.at[slot], y_recv.at[slot]
        line_start(xb, part.astype(BF16), me_x, NX, xs, xr, x_dev)
        between()
        total = line_finish(xb, NX, xs, xr)
        line_start(yb, total.astype(BF16), me_y, NY, ys, yr, y_dev)
        return line_finish(yb, NY, ys, yr)

    for copy in loads:
        copy.wait()

    for z in range(NZ):
        base = 2 * OWNED * z
        vecs[base : base + OWNED] = weights[pl.ds(base, OWNED, stride=2)]
        vecs[base + OWNED : base + 2 * OWNED] = weights[pl.ds(base + 1, OWNED, stride=2)]
    mine_at = pl.multiple_of(s * 2 * OWNED, 2 * OWNED)
    w_own[:, :HALF] = vecs[pl.ds(mine_at, OWNED)]
    w_own[:, HALF:] = vecs[pl.ds(mine_at + OWNED, OWNED)]
    direc[...] = jnp.zeros((OWNED, WIDTH), F32)
    change_out[...] = jnp.zeros((GROUPS, TILE_ROWS), F32)
    fill_forward()
    for k, copy in enumerate(pieces):
        copy.wait()
        lax.fori_loop(k * per_piece, (k + 1) * per_piece, flip_tile, 0, unroll=True)
    pl.semaphore_wait(barrier, NX + NY + NM - 3)

    def one_round(t, carry):
        opening = isinstance(t, int)
        if opening:
            summed = sum_rows(forward(), t % 2, prepare_hess)
            prob = jax.nn.sigmoid(summed)
            curv[...] = prob * (1.0 - prob)
            rows[...] = prob - labels[...].astype(F32)
        else:
            change = change_out[...] + sum_rows(forward(), t % 2, lambda: None)
            change_out[...] = change
            rows[...] = curv[...] * change

        left, right = backward()
        for z in range(NZ):
            at = slice(OWNED * z, OWNED * (z + 1))
            rs_out[z] = jnp.concatenate([left[at], right[at]], axis=0).astype(BF16)
        terms = rs_in.at[t % 2]
        for j in far_first(NM, NZ):
            dev = z_dev(j)
            send(rs_out.at[dev[1]], terms.at[me], z_send.at[0], z_recv.at[t % 2], dev)
        terms[me] = rs_out[s]
        drain(terms.at[pl.ds(0, NM - 1)], z_recv.at[t % 2])
        mine = terms[0].astype(F32)
        for k in range(1, NM):
            mine = mine + terms[k].astype(F32)
        mine = jnp.concatenate([mine[:OWNED], mine[OWNED:]], axis=1)
        drain(terms.at[pl.ds(0, NM - 1)], z_send.at[0])

        direction = direc[...]
        if opening:
            grad[...] = mine
            hess_copy.wait()
            thr_copy.wait()
            model_grad = mine
        else:
            model_grad = grad[...] + mine + ridge_term * direction
        high = model_grad.astype(BF16).astype(F32)
        pair = jnp.concatenate([high, model_grad - high], axis=0)
        at = iota((2 * OWNED, WIDTH), 0) % OWNED
        parts = [jnp.where(at == i, pair, 0.0).astype(BF16) for i in range(OWNED)]
        spread = jnp.concatenate(parts, axis=1)
        flipped = hess_t[...].reshape(OWNED * WIDTH, WIDTH)
        product = jnp.concatenate(
            [
                jnp.dot(spread, flipped[:, :HALF], preferred_element_type=F32),
                jnp.dot(spread, flipped[:, HALF:], preferred_element_type=F32),
            ],
            axis=1,
        )
        newton = product[:OWNED] + product[OWNED:]
        weight = w_own[...]
        trial = weight + direction - newton
        threshold = jnp.concatenate([thr[0], thr[1]], axis=0)
        size = jnp.maximum(jnp.abs(trial) - threshold, 0.0)
        shrunk = jnp.where(trial > 0.0, size, jnp.where(trial < 0.0, -size, 0.0))
        active = (segment[...] == t % SEGMENTS) & (t // SEGMENTS < limit[...])
        step = jnp.where(active, shrunk - weight - direction, 0.0)
        direc[...] = direction + step

        slot = ag_buf.at[s]
        slot[...] = jnp.concatenate([step[:, :HALF], step[:, HALF:]], axis=0).astype(BF16)
        for j in far_first(NZ, NZ):
            send(slot, slot, z_send.at[1], z_recv.at[2], z_same(j))
        drain(ag_buf.at[pl.ds(0, NZ - 1)], z_recv.at[2])
        vecs[...] = ag_buf[...].reshape(2 * BLOCKS, HALF).astype(F32)
        drain(ag_buf.at[pl.ds(0, NZ - 1)], z_send.at[1])
        fill_forward()
        return carry

    one_round(0, 0)
    lax.fori_loop(1, ROUNDS, one_round, 0)

    direction = direc[...]
    weight = w_own[...]
    linear = grad[...] * direction + 0.5 * ridge_term * direction * direction
    linear = linear + penalty * (jnp.abs(weight + direction) - jnp.abs(weight))
    linear = jnp.where(iota((OWNED, WIDTH), 0) // SHARE == r, linear, 0.0)
    linear = linear[:, :HALF] + linear[:, HALF:]
    slot = ROUNDS % 2
    xb, yb = x_buf.at[slot], y_buf.at[slot]
    xs, xr, ys, yr = x_send.at[slot], x_recv.at[slot], y_send.at[slot], y_recv.at[slot]
    line_start(xb, forward().astype(BF16), me_x, NX, xs, xr, x_dev)
    line_start(lx_buf, linear, me_x, NX, l_send.at[0], l_recv.at[0], x_dev)
    total = line_finish(xb, NX, xs, xr)
    line_start(yb, total.astype(BF16), me_y, NY, ys, yr, y_dev)
    linear = line_finish(lx_buf, NX, l_send.at[0], l_recv.at[0])
    line_start(ly_buf, linear, me_y, NY, l_send.at[1], l_recv.at[1], y_dev)
    change = change_out[...] + line_finish(yb, NY, ys, yr)
    linear = line_finish(ly_buf, NY, l_send.at[1], l_recv.at[1])
    quad = 0.5 * curv[...] * change * change
    for g in range(GROUPS // 8):
        linear = linear + quad[8 * g : 8 * g + 8]
    line_start(lz_buf, linear, me, NM, l_send.at[2], l_recv.at[2], z_dev)
    change_out[...] = change
    own = jnp.where(r == 0, direction[:SHARE], direction[SHARE:])
    dir_out[pl.ds(0, SHARE, stride=2)] = own[:, :HALF]
    dir_out[pl.ds(1, SHARE, stride=2)] = own[:, HALF:]
    total = line_finish(lz_buf, NM, l_send.at[2], l_recv.at[2])
    dec_out[...] = jnp.sum(jnp.sum(total, axis=0, keepdims=True), axis=1, keepdims=True)


def write_out(direction, change, dir_out, change_out):
    dir_out[...] = direction[...]
    change_out[...] = change[...]


def on_device(tiles, tile_block, tile_row, labels, weights, hess_inv, order, sweeps):
    vmem = pl.BlockSpec(memory_space=pltpu.VMEM)
    hbm = pl.BlockSpec(memory_space=pltpu.HBM)
    dma = pltpu.SemaphoreType.DMA
    direction, change, decrease = pl.pallas_call(
        body,
        out_shape=(
            jax.ShapeDtypeStruct((8, HALF), F32),
            jax.ShapeDtypeStruct((GROUPS, TILE_ROWS), F32),
            jax.ShapeDtypeStruct((1, 1), F32),
        ),
        in_specs=[hbm] * 8,
        out_specs=[vmem] * 3,
        scratch_shapes=[
            pltpu.SMEM((1, 1, SLOTS), jnp.int32),
            pltpu.SMEM((1, 1, SLOTS), jnp.int32),
            pltpu.SMEM((1, BLOCKS), jnp.int32),
            pltpu.SMEM((BLOCKS,), jnp.int32),
            pltpu.VMEM((SLOTS, TILE_ROWS, WIDTH), BF16),
            pltpu.VMEM((GROUPS, TILE_ROWS), jnp.int32),
            pltpu.VMEM((2 * BLOCKS, HALF), F32),
            pltpu.VMEM((SHARE, WIDTH, WIDTH), F32),
            pltpu.VMEM((SLOTS, WIDTH, TILE_ROWS), BF16),
            pltpu.VMEM((OWNED, WIDTH, WIDTH), BF16),
            pltpu.VMEM((2 * BLOCKS, HALF), F32),
            pltpu.VMEM((GROUPS, TILE_ROWS), F32),
            pltpu.VMEM((GROUPS, SLOTS * WIDTH), BF16),
            pltpu.VMEM((BLOCKS, SLOTS * TILE_ROWS), BF16),
            pltpu.VMEM((2, SHARE, WIDTH), F32),
            pltpu.VMEM((OWNED, WIDTH), F32),
            pltpu.VMEM((OWNED, WIDTH), F32),
            pltpu.VMEM((OWNED, WIDTH), F32),
            pltpu.VMEM((OWNED, WIDTH), jnp.int32),
            pltpu.VMEM((OWNED, WIDTH), jnp.int32),
            pltpu.VMEM((GROUPS, TILE_ROWS), F32),
            pltpu.VMEM((2, NX, GROUPS, TILE_ROWS), BF16),
            pltpu.VMEM((2, NY, GROUPS, TILE_ROWS), BF16),
            pltpu.VMEM((NZ, 2 * OWNED, HALF), BF16),
            pltpu.VMEM((2, NM, 2 * OWNED, HALF), BF16),
            pltpu.VMEM((NZ, 2 * OWNED, HALF), BF16),
            pltpu.VMEM((NX, 8, HALF), F32),
            pltpu.VMEM((NY, 8, HALF), F32),
            pltpu.VMEM((NM, 8, HALF), F32),
            dma((2,)),
            dma((2,)),
            dma((2,)),
            dma((2,)),
            dma((2,)),
            dma((3,)),
            dma((3,)),
            dma((3,)),
            dma((2,)),
            dma((2,)),
            dma((7 + PIECES,)),
        ],
        compiler_params=pltpu.CompilerParams(
            collective_id=0, has_side_effects=True, vmem_limit_bytes=60 * 1024 * 1024
        ),
    )(
        tile_block,
        tile_row,
        order,
        sweeps,
        tiles.reshape(SLOTS, TILE_ROWS, WIDTH),
        labels.reshape(GROUPS, TILE_ROWS),
        weights.reshape(2 * BLOCKS, HALF),
        hess_inv,
    )
    direction, change = pl.pallas_call(
        write_out,
        out_shape=(
            jax.ShapeDtypeStruct((8, HALF), F32),
            jax.ShapeDtypeStruct((GROUPS, TILE_ROWS), F32),
        ),
        in_specs=[vmem] * 2,
        out_specs=[vmem] * 2,
        compiler_params=pltpu.CompilerParams(vmem_limit_bytes=60 * 1024 * 1024),
    )(direction, change)
    return direction.reshape(-1), change.reshape(-1), decrease.reshape(1)


def solution(mesh):
    in_specs = (
        P("feat", ("samp", "rep"), None, None, None),
        P("feat", ("samp", "rep"), None),
        P("feat", ("samp", "rep"), None),
        P(("samp", "rep")),
        P("feat"),
        P(("feat", "samp", "rep"), None, None),
        P("feat", None),
        P("feat"),
    )
    out_specs = (P(("feat", "samp", "rep")), P(("samp", "rep")), P())
    return jax.shard_map(
        on_device, mesh=mesh, in_specs=in_specs, out_specs=out_specs, check_vma=False
    )
```

```python
import functools

import jax
import jax.numpy as jnp
from jax import lax
from jax.experimental import pallas as pl
from jax.experimental.pallas import tpu as pltpu
from jax.sharding import PartitionSpec as P

SWEEPS = 3
SEGMENTS = 2
ROUNDS = SWEEPS * SEGMENTS

NX = 4
NY = 8
NZ = 8
NM = 16
SLOTS = 32
TILE_ROWS = 128
WIDTH = 256
HALF = 128
GROUPS = 32
BLOCKS = 64
OWNED = 8
SHARE = 4
PIECES = 4

SIDE = ((1, 0), (3, 0))
ARM = ((0, 3), (0, 5), (0, 2), (0, 6), (0, 1), (0, 7))
FAR = (
    (2, 4),
    (1, 4),
    (3, 4),
    (2, 3),
    (2, 5),
    (2, 2),
    (2, 6),
    (0, 4),
    (2, 1),
    (2, 7),
    (2, 0),
)

penalty = 0.05
ridge_term = 0.1

MESH = pl.DeviceIdType.MESH
F32 = jnp.float32
BF16 = jnp.bfloat16


def far_first(count, chips):
    per = count // chips
    return sorted(range(1, count), key=lambda j: (-min(j // per, chips - j // per), -(j % per)))


def iota(shape, dim):
    return lax.broadcasted_iota(jnp.int32, shape, dim)


def body(
    tile_block_hbm,
    tile_row_hbm,
    order_hbm,
    sweeps_hbm,
    tiles_hbm,
    labels_hbm,
    weights_hbm,
    hess_hbm,
    dir_out,
    change_out,
    dec_out,
    tile_block,
    tile_row,
    order,
    sweeps,
    tiles,
    labels,
    weights,
    hess,
    tiles_t,
    hess_t,
    vecs,
    rows,
    q_buf,
    p_buf,
    thr,
    w_own,
    grad,
    direc,
    segment,
    limit,
    curv,
    x_buf,
    y_buf,
    parts_sum,
    side_buf,
    arm_buf,
    far_buf,
    rs_out,
    rs_in,
    ag_buf,
    lx_buf,
    ly_buf,
    lz_buf,
    x_send,
    x_recv,
    y_send,
    y_recv,
    n_send,
    n_recv,
    z_send,
    z_recv,
    l_send,
    l_recv,
    h_send,
    h_recv,
    load_sem,
):
    f, s, r = lax.axis_index("feat"), lax.axis_index("samp"), lax.axis_index("rep")
    me_x, me_y = f % NX, f // NX
    me = s * 2 + r

    def x_dev(j):
        return (me_y * NX + (me_x + j) % NX, s, r)

    def y_dev(j):
        return ((me_y + j) % NY * NX + me_x, s, r)

    def z_dev(j):
        return (f, (s + j // 2) % NZ, r ^ (j % 2))

    def z_same(j):
        return (f, (s + j) % NZ, r)

    def plane_dev(dx, dy):
        return ((me_y + dy) % NY * NX + (me_x + dx) % NX, s, r)

    barrier = pltpu.get_barrier_semaphore()
    for dx, dy in FAR:
        if dx and dy:
            pl.semaphore_signal(barrier, inc=1, device_id=plane_dev(dx, dy), device_id_type=MESH)
    for dev, count in ((y_dev, NY), (z_dev, NM), (x_dev, NX)):
        for j in far_first(count, min(count, 8)):
            pl.semaphore_signal(barrier, inc=1, device_id=dev(j), device_id_type=MESH)

    def load(src, dst, k):
        return pltpu.make_async_copy(src, dst, load_sem.at[k])

    loads = [
        load(tile_block_hbm, tile_block, 0),
        load(tile_row_hbm, tile_row, 1),
        load(weights_hbm, weights, 2),
    ]
    per_piece = SLOTS // PIECES
    pieces = [
        load(
            tiles_hbm.at[pl.ds(k * per_piece, per_piece)],
            tiles.at[pl.ds(k * per_piece, per_piece)],
            3 + k,
        )
        for k in range(PIECES)
    ]
    later = [
        load(hess_hbm, hess, 3 + PIECES),
        load(labels_hbm, labels, 4 + PIECES),
        load(order_hbm, order, 5 + PIECES),
        load(sweeps_hbm, sweeps, 6 + PIECES),
    ]
    for copy in loads + pieces + later:
        copy.start()

    row_iota = iota((GROUPS, HALF), 0)
    block_iota = iota((BLOCKS, TILE_ROWS), 0)

    def fill_forward():
        def fill(c, carry):
            b = tile_block[0, 0, c]
            live = b >= 0
            b = jnp.maximum(b, 0)
            at = 2 * OWNED * (b // OWNED) + b % OWNED
            group = jnp.where(live, tile_row[0, 0, c], -1)
            hot = row_iota == group
            left = jnp.where(hot, vecs[pl.ds(at, 1)], 0.0).astype(BF16)
            right = jnp.where(hot, vecs[pl.ds(at + OWNED, 1)], 0.0).astype(BF16)
            base = pl.multiple_of(c * WIDTH, WIDTH)
            q_buf[:, pl.ds(base, HALF)] = left
            q_buf[:, pl.ds(base + HALF, HALF)] = right
            return carry

        lax.fori_loop(0, SLOTS, fill, 0, unroll=True)

    def forward():
        flipped = tiles_t[...].reshape(SLOTS * WIDTH, TILE_ROWS)
        return jnp.dot(q_buf[...], flipped, preferred_element_type=F32)

    def backward():
        def fill(c, carry):
            b = tile_block[0, 0, c]
            picked = rows[pl.ds(tile_row[0, 0, c], 1)]
            base = pl.multiple_of(c * TILE_ROWS, TILE_ROWS)
            p_buf[:, pl.ds(base, TILE_ROWS)] = jnp.where(block_iota == b, picked, 0.0).astype(BF16)
            return carry

        lax.fori_loop(0, SLOTS, fill, 0, unroll=True)
        flat = tiles[...].reshape(SLOTS * TILE_ROWS, WIDTH)
        left = jnp.dot(p_buf[...], flat[:, :HALF], preferred_element_type=F32)
        right = jnp.dot(p_buf[...], flat[:, HALF:], preferred_element_type=F32)
        return left, right

    def remote(src, dst, send_sem, recv_sem, dev):
        return pltpu.make_async_remote_copy(
            src_ref=src,
            dst_ref=dst,
            send_sem=send_sem,
            recv_sem=recv_sem,
            device_id=dev,
            device_id_type=MESH,
        )

    def send(src, dst, send_sem, recv_sem, dev):
        remote(src, dst, send_sem, recv_sem, dev).start()

    def drain(ref, sem):
        pltpu.make_async_copy(ref, ref, sem).wait()

    def line_start(buf, value, me_at, count, send_sem, recv_sem, dev):
        buf[me_at] = value
        for j in far_first(count, min(count, 8)):
            send(buf.at[me_at], buf.at[me_at], send_sem, recv_sem, dev(j))

    def line_finish(buf, count, send_sem, recv_sem):
        drain(buf.at[pl.ds(0, count - 1)], recv_sem)
        total = buf[0].astype(F32)
        for k in range(1, count):
            total = total + buf[k].astype(F32)
        drain(buf.at[pl.ds(0, count - 1)], send_sem)
        return total

    def flip_tile(c, carry):
        tiles_t[c] = tiles[c].T
        return carry

    sibling = (f, s, 1 - r)
    own_rows = pl.ds(r * SHARE, SHARE)
    hess_copy = remote(
        hess_t.at[own_rows], hess_t.at[own_rows], h_send.at[0], h_recv.at[0], sibling
    )
    thr_copy = remote(thr.at[r], thr.at[r], h_send.at[1], h_recv.at[1], sibling)

    def prepare_hess():
        for copy in later:
            copy.wait()

        def flip_hess(i, carry):
            block = hess[i]
            hess_t[r * SHARE + i] = block.T.astype(BF16)
            on_diag = iota((WIDTH, WIDTH), 0) == iota((WIDTH, WIDTH), 1)
            diagonal = jnp.sum(jnp.where(on_diag, block, 0.0), axis=0, keepdims=True)
            thr[r, pl.ds(i, 1), :] = penalty * diagonal
            return carry

        lax.fori_loop(0, SHARE, flip_hess, 0)
        hess_copy.start()
        thr_copy.start()
        sub = iota((OWNED, WIDTH), 0)

        def find(p, found):
            return found + jnp.where(order[0, p] == s * OWNED + sub, 1, 0)

        first = lax.fori_loop(
            0, BLOCKS // SEGMENTS, find, jnp.zeros((OWNED, WIDTH), jnp.int32), unroll=True
        )
        segment[...] = 1 - first
        most = jnp.zeros((OWNED, WIDTH), jnp.int32)
        for i in range(OWNED):
            most = jnp.where(sub == i, sweeps[s * OWNED + i], most)
        limit[...] = most

    def sum_rows(part, slot, between):
        xb, yb = x_buf.at[slot], y_buf.at[slot]
        xs, xr, ys, yr = x_send.at[slot], x_recv.at[slot], y_send.at[slot], y_recv.at[slot]
        line_start(xb, part.astype(BF16), me_x, NX, xs, xr, x_dev)
        between()
        total = line_finish(xb, NX, xs, xr)
        line_start(yb, total.astype(BF16), me_y, NY, ys, yr, y_dev)
        return line_finish(yb, NY, ys, yr)

    def near_sum(part, slot):
        side, arm, far = side_buf.at[slot], arm_buf.at[slot], far_buf.at[slot]
        stages = ((side, SIDE, 0), (arm, ARM, 1), (far, FAR, 2))

        def start(stage, value):
            buf, offsets, k = stage
            last = len(offsets)
            buf[last] = value.astype(BF16)
            for j, (dx, dy) in enumerate(offsets):
                send(buf.at[last], buf.at[j], n_send.at[slot, k], n_recv.at[slot, k], plane_dev(dx, dy))

        def finish(stage, total):
            buf, offsets, k = stage
            got = buf.at[pl.ds(0, len(offsets))]
            drain(got, n_recv.at[slot, k])
            for j in range(len(offsets)):
                total = total + buf[j].astype(F32)
            drain(got, n_send.at[slot, k])
            return total

        start(stages[0], part)
        start(stages[2], part)
        triple = finish(stages[0], part)
        start(stages[1], triple)
        total = finish(stages[2], triple)
        return finish(stages[1], total)

    for copy in loads:
        copy.wait()

    for z in range(NZ):
        base = 2 * OWNED * z
        vecs[base : base + OWNED] = weights[pl.ds(base, OWNED, stride=2)]
        vecs[base + OWNED : base + 2 * OWNED] = weights[pl.ds(base + 1, OWNED, stride=2)]
    mine_at = pl.multiple_of(s * 2 * OWNED, 2 * OWNED)
    w_own[:, :HALF] = vecs[pl.ds(mine_at, OWNED)]
    w_own[:, HALF:] = vecs[pl.ds(mine_at + OWNED, OWNED)]
    direc[...] = jnp.zeros((OWNED, WIDTH), F32)
    change_out[...] = jnp.zeros((GROUPS, TILE_ROWS), F32)
    parts_sum[...] = jnp.zeros((GROUPS, TILE_ROWS), F32)
    fill_forward()
    for k, copy in enumerate(pieces):
        copy.wait()
        lax.fori_loop(k * per_piece, (k + 1) * per_piece, flip_tile, 0, unroll=True)
    pl.semaphore_wait(barrier, NX + NY + NM - 3 + sum(1 for dx, dy in FAR if dx and dy))

    def one_round(t, carry):
        opening = isinstance(t, int)
        if opening:
            summed = sum_rows(forward(), t % 2, prepare_hess)
            prob = jax.nn.sigmoid(summed)
            curv[...] = prob * (1.0 - prob)
            rows[...] = prob - labels[...].astype(F32)
        else:
            part = forward()
            parts_sum[...] += part
            change = change_out[...] + near_sum(part, t % 2)
            change_out[...] = change
            rows[...] = curv[...] * change

        left, right = backward()
        for z in range(NZ):
            at = slice(OWNED * z, OWNED * (z + 1))
            rs_out[z] = jnp.concatenate([left[at], right[at]], axis=0).astype(BF16)
        terms = rs_in.at[t % 2]
        for j in far_first(NM, NZ):
            dev = z_dev(j)
            send(rs_out.at[dev[1]], terms.at[me], z_send.at[0], z_recv.at[t % 2], dev)
        terms[me] = rs_out[s]
        drain(terms.at[pl.ds(0, NM - 1)], z_recv.at[t % 2])
        mine = terms[0].astype(F32)
        for k in range(1, NM):
            mine = mine + terms[k].astype(F32)
        mine = jnp.concatenate([mine[:OWNED], mine[OWNED:]], axis=1)
        drain(terms.at[pl.ds(0, NM - 1)], z_send.at[0])

        direction = direc[...]
        if opening:
            grad[...] = mine
            hess_copy.wait()
            thr_copy.wait()
            model_grad = mine
        else:
            model_grad = grad[...] + mine + ridge_term * direction
        high = model_grad.astype(BF16).astype(F32)
        pair = jnp.concatenate([high, model_grad - high], axis=0)
        at = iota((2 * OWNED, WIDTH), 0) % OWNED
        parts = [jnp.where(at == i, pair, 0.0).astype(BF16) for i in range(OWNED)]
        spread = jnp.concatenate(parts, axis=1)
        flipped = hess_t[...].reshape(OWNED * WIDTH, WIDTH)
        product = jnp.concatenate(
            [
                jnp.dot(spread, flipped[:, :HALF], preferred_element_type=F32),
                jnp.dot(spread, flipped[:, HALF:], preferred_element_type=F32),
            ],
            axis=1,
        )
        newton = product[:OWNED] + product[OWNED:]
        weight = w_own[...]
        trial = weight + direction - newton
        threshold = jnp.concatenate([thr[0], thr[1]], axis=0)
        size = jnp.maximum(jnp.abs(trial) - threshold, 0.0)
        shrunk = jnp.where(trial > 0.0, size, jnp.where(trial < 0.0, -size, 0.0))
        active = (segment[...] == t % SEGMENTS) & (t // SEGMENTS < limit[...])
        step = jnp.where(active, shrunk - weight - direction, 0.0)
        direc[...] = direction + step

        slot = ag_buf.at[s]
        slot[...] = jnp.concatenate([step[:, :HALF], step[:, HALF:]], axis=0).astype(BF16)
        for j in far_first(NZ, NZ):
            send(slot, slot, z_send.at[1], z_recv.at[2], z_same(j))
        drain(ag_buf.at[pl.ds(0, NZ - 1)], z_recv.at[2])
        vecs[...] = ag_buf[...].reshape(2 * BLOCKS, HALF).astype(F32)
        drain(ag_buf.at[pl.ds(0, NZ - 1)], z_send.at[1])
        fill_forward()
        return carry

    one_round(0, 0)
    lax.fori_loop(1, ROUNDS, one_round, 0)

    direction = direc[...]
    weight = w_own[...]
    linear = grad[...] * direction + 0.5 * ridge_term * direction * direction
    linear = linear + penalty * (jnp.abs(weight + direction) - jnp.abs(weight))
    linear = jnp.where(iota((OWNED, WIDTH), 0) // SHARE == r, linear, 0.0)
    linear = linear[:, :HALF] + linear[:, HALF:]
    slot = 1
    xb, yb = x_buf.at[slot], y_buf.at[slot]
    xs, xr, ys, yr = x_send.at[slot], x_recv.at[slot], y_send.at[slot], y_recv.at[slot]
    line_start(xb, (parts_sum[...] + forward()).astype(BF16), me_x, NX, xs, xr, x_dev)
    line_start(lx_buf, linear, me_x, NX, l_send.at[0], l_recv.at[0], x_dev)
    total = line_finish(xb, NX, xs, xr)
    line_start(yb, total.astype(BF16), me_y, NY, ys, yr, y_dev)
    linear = line_finish(lx_buf, NX, l_send.at[0], l_recv.at[0])
    line_start(ly_buf, linear, me_y, NY, l_send.at[1], l_recv.at[1], y_dev)
    change = line_finish(yb, NY, ys, yr)
    linear = line_finish(ly_buf, NY, l_send.at[1], l_recv.at[1])
    quad = 0.5 * curv[...] * change * change
    for g in range(GROUPS // 8):
        linear = linear + quad[8 * g : 8 * g + 8]
    line_start(lz_buf, linear, me, NM, l_send.at[2], l_recv.at[2], z_dev)
    change_out[...] = change
    own = jnp.where(r == 0, direction[:SHARE], direction[SHARE:])
    dir_out[pl.ds(0, SHARE, stride=2)] = own[:, :HALF]
    dir_out[pl.ds(1, SHARE, stride=2)] = own[:, HALF:]
    total = line_finish(lz_buf, NM, l_send.at[2], l_recv.at[2])
    dec_out[...] = jnp.sum(jnp.sum(total, axis=0, keepdims=True), axis=1, keepdims=True)


def write_out(direction, change, dir_out, change_out):
    dir_out[...] = direction[...]
    change_out[...] = change[...]


def on_device(tiles, tile_block, tile_row, labels, weights, hess_inv, order, sweeps):
    vmem = pl.BlockSpec(memory_space=pltpu.VMEM)
    hbm = pl.BlockSpec(memory_space=pltpu.HBM)
    dma = pltpu.SemaphoreType.DMA
    direction, change, decrease = pl.pallas_call(
        body,
        out_shape=(
            jax.ShapeDtypeStruct((8, HALF), F32),
            jax.ShapeDtypeStruct((GROUPS, TILE_ROWS), F32),
            jax.ShapeDtypeStruct((1, 1), F32),
        ),
        in_specs=[hbm] * 8,
        out_specs=[vmem] * 3,
        scratch_shapes=[
            pltpu.SMEM((1, 1, SLOTS), jnp.int32),
            pltpu.SMEM((1, 1, SLOTS), jnp.int32),
            pltpu.SMEM((1, BLOCKS), jnp.int32),
            pltpu.SMEM((BLOCKS,), jnp.int32),
            pltpu.VMEM((SLOTS, TILE_ROWS, WIDTH), BF16),
            pltpu.VMEM((GROUPS, TILE_ROWS), jnp.int32),
            pltpu.VMEM((2 * BLOCKS, HALF), F32),
            pltpu.VMEM((SHARE, WIDTH, WIDTH), F32),
            pltpu.VMEM((SLOTS, WIDTH, TILE_ROWS), BF16),
            pltpu.VMEM((OWNED, WIDTH, WIDTH), BF16),
            pltpu.VMEM((2 * BLOCKS, HALF), F32),
            pltpu.VMEM((GROUPS, TILE_ROWS), F32),
            pltpu.VMEM((GROUPS, SLOTS * WIDTH), BF16),
            pltpu.VMEM((BLOCKS, SLOTS * TILE_ROWS), BF16),
            pltpu.VMEM((2, SHARE, WIDTH), F32),
            pltpu.VMEM((OWNED, WIDTH), F32),
            pltpu.VMEM((OWNED, WIDTH), F32),
            pltpu.VMEM((OWNED, WIDTH), F32),
            pltpu.VMEM((OWNED, WIDTH), jnp.int32),
            pltpu.VMEM((OWNED, WIDTH), jnp.int32),
            pltpu.VMEM((GROUPS, TILE_ROWS), F32),
            pltpu.VMEM((2, NX, GROUPS, TILE_ROWS), BF16),
            pltpu.VMEM((2, NY, GROUPS, TILE_ROWS), BF16),
            pltpu.VMEM((GROUPS, TILE_ROWS), F32),
            pltpu.VMEM((2, len(SIDE) + 1, GROUPS, TILE_ROWS), BF16),
            pltpu.VMEM((2, len(ARM) + 1, GROUPS, TILE_ROWS), BF16),
            pltpu.VMEM((2, len(FAR) + 1, GROUPS, TILE_ROWS), BF16),
            pltpu.VMEM((NZ, 2 * OWNED, HALF), BF16),
            pltpu.VMEM((2, NM, 2 * OWNED, HALF), BF16),
            pltpu.VMEM((NZ, 2 * OWNED, HALF), BF16),
            pltpu.VMEM((NX, 8, HALF), F32),
            pltpu.VMEM((NY, 8, HALF), F32),
            pltpu.VMEM((NM, 8, HALF), F32),
            dma((2,)),
            dma((2,)),
            dma((2,)),
            dma((2,)),
            dma((2, 3)),
            dma((2, 3)),
            dma((2,)),
            dma((3,)),
            dma((3,)),
            dma((3,)),
            dma((2,)),
            dma((2,)),
            dma((7 + PIECES,)),
        ],
        compiler_params=pltpu.CompilerParams(
            collective_id=0, has_side_effects=True, vmem_limit_bytes=60 * 1024 * 1024
        ),
    )(
        tile_block,
        tile_row,
        order,
        sweeps,
        tiles.reshape(SLOTS, TILE_ROWS, WIDTH),
        labels.reshape(GROUPS, TILE_ROWS),
        weights.reshape(2 * BLOCKS, HALF),
        hess_inv,
    )
    direction, change = pl.pallas_call(
        write_out,
        out_shape=(
            jax.ShapeDtypeStruct((8, HALF), F32),
            jax.ShapeDtypeStruct((GROUPS, TILE_ROWS), F32),
        ),
        in_specs=[vmem] * 2,
        out_specs=[vmem] * 2,
        compiler_params=pltpu.CompilerParams(vmem_limit_bytes=60 * 1024 * 1024),
    )(direction, change)
    return direction.reshape(-1), change.reshape(-1), decrease.reshape(1)


def solution(mesh):
    in_specs = (
        P("feat", ("samp", "rep"), None, None, None),
        P("feat", ("samp", "rep"), None),
        P("feat", ("samp", "rep"), None),
        P(("samp", "rep")),
        P("feat"),
        P(("feat", "samp", "rep"), None, None),
        P("feat", None),
        P("feat"),
    )
    out_specs = (P(("feat", "samp", "rep")), P(("samp", "rep")), P())
    return jax.shard_map(
        on_device, mesh=mesh, in_specs=in_specs, out_specs=out_specs, check_vma=False
    )
```

```python
import functools

import jax
import jax.numpy as jnp
from jax import lax
from jax.experimental import pallas as pl
from jax.experimental.pallas import tpu as pltpu
from jax.sharding import PartitionSpec as P

SWEEPS = 3
SEGMENTS = 2
ROUNDS = SWEEPS * SEGMENTS

NX = 4
NY = 8
NZ = 8
NM = 16
SLOTS = 32
TILE_ROWS = 128
WIDTH = 256
HALF = 128
GROUPS = 32
BLOCKS = 64
OWNED = 8
SHARE = 4
PIECES = 4

SIDE = ((1, 0), (3, 0))
ARM = ((0, 3), (0, 5), (0, 2), (0, 6), (0, 1), (0, 7))
FAR = (
    (2, 4),
    (1, 4),
    (3, 4),
    (2, 3),
    (2, 5),
    (2, 2),
    (2, 6),
    (0, 4),
    (2, 1),
    (2, 7),
    (2, 0),
)

penalty = 0.05
ridge_term = 0.1

MESH = pl.DeviceIdType.MESH
F32 = jnp.float32
BF16 = jnp.bfloat16


def far_first(count, chips):
    per = count // chips
    return sorted(range(1, count), key=lambda j: (-min(j // per, chips - j // per), -(j % per)))


def iota(shape, dim):
    return lax.broadcasted_iota(jnp.int32, shape, dim)


def body(
    tile_block_hbm,
    tile_row_hbm,
    order_hbm,
    sweeps_hbm,
    tiles_hbm,
    labels_hbm,
    weights_hbm,
    hess_hbm,
    dir_out,
    change_out,
    dec_out,
    tile_block,
    tile_row,
    order,
    sweeps,
    tiles,
    labels,
    weights,
    hess,
    tiles_t,
    hess_t,
    vecs,
    rows,
    q_buf,
    p_buf,
    thr,
    w_own,
    grad,
    direc,
    segment,
    limit,
    curv,
    x_buf,
    y_buf,
    parts_sum,
    side_buf,
    arm_buf,
    far_buf,
    rs_out,
    rs_in,
    ag_buf,
    lx_buf,
    ly_buf,
    lz_buf,
    x_send,
    x_recv,
    y_send,
    y_recv,
    n_send,
    n_recv,
    z_send,
    z_recv,
    l_send,
    l_recv,
    h_send,
    h_recv,
    load_sem,
):
    f, s, r = lax.axis_index("feat"), lax.axis_index("samp"), lax.axis_index("rep")
    me_x, me_y = f % NX, f // NX
    me = s * 2 + r

    def x_dev(j):
        return (me_y * NX + (me_x + j) % NX, s, r)

    def y_dev(j):
        return ((me_y + j) % NY * NX + me_x, s, r)

    def z_dev(j):
        return (f, (s + j // 2) % NZ, r ^ (j % 2))

    def z_same(j):
        return (f, (s + j) % NZ, r)

    def plane_dev(dx, dy):
        return ((me_y + dy) % NY * NX + (me_x + dx) % NX, s, r)

    barrier = pltpu.get_barrier_semaphore()
    for dx, dy in FAR:
        if dx and dy:
            pl.semaphore_signal(barrier, inc=1, device_id=plane_dev(dx, dy), device_id_type=MESH)
    for dev, count in ((y_dev, NY), (z_dev, NM), (x_dev, NX)):
        for j in far_first(count, min(count, 8)):
            pl.semaphore_signal(barrier, inc=1, device_id=dev(j), device_id_type=MESH)

    def load(src, dst, k):
        return pltpu.make_async_copy(src, dst, load_sem.at[k])

    loads = [
        load(tile_block_hbm, tile_block, 0),
        load(tile_row_hbm, tile_row, 1),
        load(weights_hbm, weights, 2),
    ]
    per_piece = SLOTS // PIECES
    pieces = [
        load(
            tiles_hbm.at[pl.ds(k * per_piece, per_piece)],
            tiles.at[pl.ds(k * per_piece, per_piece)],
            3 + k,
        )
        for k in range(PIECES)
    ]
    later = [
        load(hess_hbm, hess, 3 + PIECES),
        load(labels_hbm, labels, 4 + PIECES),
        load(order_hbm, order, 5 + PIECES),
        load(sweeps_hbm, sweeps, 6 + PIECES),
    ]
    for copy in loads + pieces + later:
        copy.start()

    row_iota = iota((GROUPS, HALF), 0)
    block_iota = iota((BLOCKS, TILE_ROWS), 0)

    def fill_forward():
        def fill(c, carry):
            b = tile_block[0, 0, c]
            live = b >= 0
            b = jnp.maximum(b, 0)
            at = 2 * OWNED * (b // OWNED) + b % OWNED
            group = jnp.where(live, tile_row[0, 0, c], -1)
            hot = row_iota == group
            left = jnp.where(hot, vecs[pl.ds(at, 1)], 0.0).astype(BF16)
            right = jnp.where(hot, vecs[pl.ds(at + OWNED, 1)], 0.0).astype(BF16)
            base = pl.multiple_of(c * WIDTH, WIDTH)
            q_buf[:, pl.ds(base, HALF)] = left
            q_buf[:, pl.ds(base + HALF, HALF)] = right
            return carry

        lax.fori_loop(0, SLOTS, fill, 0, unroll=True)

    def forward():
        flipped = tiles_t[...].reshape(SLOTS * WIDTH, TILE_ROWS)
        return jnp.dot(q_buf[...], flipped, preferred_element_type=F32)

    def backward():
        def fill(c, carry):
            b = tile_block[0, 0, c]
            picked = rows[pl.ds(tile_row[0, 0, c], 1)]
            base = pl.multiple_of(c * TILE_ROWS, TILE_ROWS)
            p_buf[:, pl.ds(base, TILE_ROWS)] = jnp.where(block_iota == b, picked, 0.0).astype(BF16)
            return carry

        lax.fori_loop(0, SLOTS, fill, 0, unroll=True)
        flat = tiles[...].reshape(SLOTS * TILE_ROWS, WIDTH)
        left = jnp.dot(p_buf[...], flat[:, :HALF], preferred_element_type=F32)
        right = jnp.dot(p_buf[...], flat[:, HALF:], preferred_element_type=F32)
        return left, right

    def remote(src, dst, send_sem, recv_sem, dev):
        return pltpu.make_async_remote_copy(
            src_ref=src,
            dst_ref=dst,
            send_sem=send_sem,
            recv_sem=recv_sem,
            device_id=dev,
            device_id_type=MESH,
        )

    def send(src, dst, send_sem, recv_sem, dev):
        remote(src, dst, send_sem, recv_sem, dev).start()

    def drain(ref, sem):
        pltpu.make_async_copy(ref, ref, sem).wait()

    def line_start(buf, value, me_at, count, send_sem, recv_sem, dev):
        buf[me_at] = value
        for j in far_first(count, min(count, 8)):
            send(buf.at[me_at], buf.at[me_at], send_sem, recv_sem, dev(j))

    def line_finish(buf, count, send_sem, recv_sem):
        drain(buf.at[pl.ds(0, count - 1)], recv_sem)
        total = buf[0].astype(F32)
        for k in range(1, count):
            total = total + buf[k].astype(F32)
        drain(buf.at[pl.ds(0, count - 1)], send_sem)
        return total

    def flip_tile(c, carry):
        tiles_t[c] = tiles[c].T
        return carry

    sibling = (f, s, 1 - r)
    own_rows = pl.ds(r * SHARE, SHARE)
    hess_copy = remote(
        hess_t.at[own_rows], hess_t.at[own_rows], h_send.at[0], h_recv.at[0], sibling
    )
    thr_copy = remote(thr.at[r], thr.at[r], h_send.at[1], h_recv.at[1], sibling)

    def prepare_hess():
        for copy in later:
            copy.wait()

        def flip_hess(i, carry):
            block = hess[i]
            hess_t[r * SHARE + i] = block.T.astype(BF16)
            on_diag = iota((WIDTH, WIDTH), 0) == iota((WIDTH, WIDTH), 1)
            diagonal = jnp.sum(jnp.where(on_diag, block, 0.0), axis=0, keepdims=True)
            thr[r, pl.ds(i, 1), :] = penalty * diagonal
            return carry

        lax.fori_loop(0, SHARE, flip_hess, 0)
        hess_copy.start()
        thr_copy.start()
        sub = iota((OWNED, WIDTH), 0)

        def find(p, found):
            return found + jnp.where(order[0, p] == s * OWNED + sub, 1, 0)

        first = lax.fori_loop(
            0, BLOCKS // SEGMENTS, find, jnp.zeros((OWNED, WIDTH), jnp.int32), unroll=True
        )
        segment[...] = 1 - first
        most = jnp.zeros((OWNED, WIDTH), jnp.int32)
        for i in range(OWNED):
            most = jnp.where(sub == i, sweeps[s * OWNED + i], most)
        limit[...] = most

    def sum_rows(part, slot, between):
        xb, yb = x_buf.at[slot], y_buf.at[slot]
        xs, xr, ys, yr = x_send.at[slot], x_recv.at[slot], y_send.at[slot], y_recv.at[slot]
        line_start(xb, part.astype(BF16), me_x, NX, xs, xr, x_dev)
        between()
        total = line_finish(xb, NX, xs, xr)
        line_start(yb, total.astype(BF16), me_y, NY, ys, yr, y_dev)
        return line_finish(yb, NY, ys, yr)

    def near_sum(part, slot):
        side, arm, far = side_buf.at[slot], arm_buf.at[slot], far_buf.at[slot]
        stages = ((side, SIDE, 0), (arm, ARM, 1), (far, FAR, 2))

        def start(stage, value):
            buf, offsets, k = stage
            last = len(offsets)
            buf[last] = value.astype(BF16)
            for j, (dx, dy) in enumerate(offsets):
                send(buf.at[last], buf.at[j], n_send.at[slot, k], n_recv.at[slot, k], plane_dev(dx, dy))

        def finish(stage, total):
            buf, offsets, k = stage
            got = buf.at[pl.ds(0, len(offsets))]
            drain(got, n_recv.at[slot, k])
            for j in range(len(offsets)):
                total = total + buf[j].astype(F32)
            drain(got, n_send.at[slot, k])
            return total

        start(stages[0], part)
        start(stages[2], part)
        triple = finish(stages[0], part)
        start(stages[1], triple)
        total = finish(stages[2], triple)
        return finish(stages[1], total)

    for copy in loads:
        copy.wait()

    for z in range(NZ):
        base = 2 * OWNED * z
        vecs[base : base + OWNED] = weights[pl.ds(base, OWNED, stride=2)]
        vecs[base + OWNED : base + 2 * OWNED] = weights[pl.ds(base + 1, OWNED, stride=2)]
    mine_at = pl.multiple_of(s * 2 * OWNED, 2 * OWNED)
    w_own[:, :HALF] = vecs[pl.ds(mine_at, OWNED)]
    w_own[:, HALF:] = vecs[pl.ds(mine_at + OWNED, OWNED)]
    direc[...] = jnp.zeros((OWNED, WIDTH), F32)
    change_out[...] = jnp.zeros((GROUPS, TILE_ROWS), F32)
    parts_sum[...] = jnp.zeros((GROUPS, TILE_ROWS), F32)
    fill_forward()
    for k, copy in enumerate(pieces):
        copy.wait()
        lax.fori_loop(k * per_piece, (k + 1) * per_piece, flip_tile, 0, unroll=True)
    pl.semaphore_wait(barrier, NX + NY + NM - 3 + sum(1 for dx, dy in FAR if dx and dy))

    def one_round(t, carry):
        opening = t == 0
        if opening:
            summed = sum_rows(forward(), t % 2, prepare_hess)
            prob = jax.nn.sigmoid(summed)
            curv[...] = prob * (1.0 - prob)
            rows[...] = prob - labels[...].astype(F32)
        else:
            part = forward()
            parts_sum[...] += part
            change = change_out[...] + near_sum(part, t % 2)
            change_out[...] = change
            rows[...] = curv[...] * change

        left, right = backward()
        for z in range(NZ):
            at = slice(OWNED * z, OWNED * (z + 1))
            rs_out[z] = jnp.concatenate([left[at], right[at]], axis=0).astype(BF16)
        terms = rs_in.at[t % 2]
        for j in far_first(NM, NZ):
            dev = z_dev(j)
            send(rs_out.at[dev[1]], terms.at[me], z_send.at[0], z_recv.at[t % 2], dev)
        terms[me] = rs_out[s]
        drain(terms.at[pl.ds(0, NM - 1)], z_recv.at[t % 2])
        mine = terms[0].astype(F32)
        for k in range(1, NM):
            mine = mine + terms[k].astype(F32)
        mine = jnp.concatenate([mine[:OWNED], mine[OWNED:]], axis=1)
        drain(terms.at[pl.ds(0, NM - 1)], z_send.at[0])

        direction = direc[...]
        if opening:
            grad[...] = mine
            hess_copy.wait()
            thr_copy.wait()
            model_grad = mine
        else:
            model_grad = grad[...] + mine + ridge_term * direction
        high = model_grad.astype(BF16).astype(F32)
        pair = jnp.concatenate([high, model_grad - high], axis=0)
        at = iota((2 * OWNED, WIDTH), 0) % OWNED
        parts = [jnp.where(at == i, pair, 0.0).astype(BF16) for i in range(OWNED)]
        spread = jnp.concatenate(parts, axis=1)
        flipped = hess_t[...].reshape(OWNED * WIDTH, WIDTH)
        product = jnp.concatenate(
            [
                jnp.dot(spread, flipped[:, :HALF], preferred_element_type=F32),
                jnp.dot(spread, flipped[:, HALF:], preferred_element_type=F32),
            ],
            axis=1,
        )
        newton = product[:OWNED] + product[OWNED:]
        weight = w_own[...]
        trial = weight + direction - newton
        threshold = jnp.concatenate([thr[0], thr[1]], axis=0)
        size = jnp.maximum(jnp.abs(trial) - threshold, 0.0)
        shrunk = jnp.where(trial > 0.0, size, jnp.where(trial < 0.0, -size, 0.0))
        active = (segment[...] == t % SEGMENTS) & (t // SEGMENTS < limit[...])
        step = jnp.where(active, shrunk - weight - direction, 0.0)
        direc[...] = direction + step

        slot = ag_buf.at[s]
        slot[...] = jnp.concatenate([step[:, :HALF], step[:, HALF:]], axis=0).astype(BF16)
        for j in far_first(NZ, NZ):
            send(slot, slot, z_send.at[1], z_recv.at[2], z_same(j))
        drain(ag_buf.at[pl.ds(0, NZ - 1)], z_recv.at[2])
        vecs[...] = ag_buf[...].reshape(2 * BLOCKS, HALF).astype(F32)
        drain(ag_buf.at[pl.ds(0, NZ - 1)], z_send.at[1])
        fill_forward()
        return carry

    for t in range(ROUNDS):
        one_round(t, 0)

    direction = direc[...]
    weight = w_own[...]
    linear = grad[...] * direction + 0.5 * ridge_term * direction * direction
    linear = linear + penalty * (jnp.abs(weight + direction) - jnp.abs(weight))
    linear = jnp.where(iota((OWNED, WIDTH), 0) // SHARE == r, linear, 0.0)
    linear = linear[:, :HALF] + linear[:, HALF:]
    slot = 1
    xb, yb = x_buf.at[slot], y_buf.at[slot]
    xs, xr, ys, yr = x_send.at[slot], x_recv.at[slot], y_send.at[slot], y_recv.at[slot]
    line_start(xb, (parts_sum[...] + forward()).astype(BF16), me_x, NX, xs, xr, x_dev)
    line_start(lx_buf, linear, me_x, NX, l_send.at[0], l_recv.at[0], x_dev)
    total = line_finish(xb, NX, xs, xr)
    line_start(yb, total.astype(BF16), me_y, NY, ys, yr, y_dev)
    linear = line_finish(lx_buf, NX, l_send.at[0], l_recv.at[0])
    line_start(ly_buf, linear, me_y, NY, l_send.at[1], l_recv.at[1], y_dev)
    change = line_finish(yb, NY, ys, yr)
    linear = line_finish(ly_buf, NY, l_send.at[1], l_recv.at[1])
    quad = 0.5 * curv[...] * change * change
    for g in range(GROUPS // 8):
        linear = linear + quad[8 * g : 8 * g + 8]
    line_start(lz_buf, linear, me, NM, l_send.at[2], l_recv.at[2], z_dev)
    change_out[...] = change
    own = jnp.where(r == 0, direction[:SHARE], direction[SHARE:])
    dir_out[pl.ds(0, SHARE, stride=2)] = own[:, :HALF]
    dir_out[pl.ds(1, SHARE, stride=2)] = own[:, HALF:]
    total = line_finish(lz_buf, NM, l_send.at[2], l_recv.at[2])
    dec_out[...] = jnp.sum(jnp.sum(total, axis=0, keepdims=True), axis=1, keepdims=True)


def write_out(direction, change, dir_out, change_out):
    dir_out[...] = direction[...]
    change_out[...] = change[...]


def on_device(tiles, tile_block, tile_row, labels, weights, hess_inv, order, sweeps):
    vmem = pl.BlockSpec(memory_space=pltpu.VMEM)
    hbm = pl.BlockSpec(memory_space=pltpu.HBM)
    dma = pltpu.SemaphoreType.DMA
    direction, change, decrease = pl.pallas_call(
        body,
        out_shape=(
            jax.ShapeDtypeStruct((8, HALF), F32),
            jax.ShapeDtypeStruct((GROUPS, TILE_ROWS), F32),
            jax.ShapeDtypeStruct((1, 1), F32),
        ),
        in_specs=[hbm] * 8,
        out_specs=[vmem] * 3,
        scratch_shapes=[
            pltpu.SMEM((1, 1, SLOTS), jnp.int32),
            pltpu.SMEM((1, 1, SLOTS), jnp.int32),
            pltpu.SMEM((1, BLOCKS), jnp.int32),
            pltpu.SMEM((BLOCKS,), jnp.int32),
            pltpu.VMEM((SLOTS, TILE_ROWS, WIDTH), BF16),
            pltpu.VMEM((GROUPS, TILE_ROWS), jnp.int32),
            pltpu.VMEM((2 * BLOCKS, HALF), F32),
            pltpu.VMEM((SHARE, WIDTH, WIDTH), F32),
            pltpu.VMEM((SLOTS, WIDTH, TILE_ROWS), BF16),
            pltpu.VMEM((OWNED, WIDTH, WIDTH), BF16),
            pltpu.VMEM((2 * BLOCKS, HALF), F32),
            pltpu.VMEM((GROUPS, TILE_ROWS), F32),
            pltpu.VMEM((GROUPS, SLOTS * WIDTH), BF16),
            pltpu.VMEM((BLOCKS, SLOTS * TILE_ROWS), BF16),
            pltpu.VMEM((2, SHARE, WIDTH), F32),
            pltpu.VMEM((OWNED, WIDTH), F32),
            pltpu.VMEM((OWNED, WIDTH), F32),
            pltpu.VMEM((OWNED, WIDTH), F32),
            pltpu.VMEM((OWNED, WIDTH), jnp.int32),
            pltpu.VMEM((OWNED, WIDTH), jnp.int32),
            pltpu.VMEM((GROUPS, TILE_ROWS), F32),
            pltpu.VMEM((2, NX, GROUPS, TILE_ROWS), BF16),
            pltpu.VMEM((2, NY, GROUPS, TILE_ROWS), BF16),
            pltpu.VMEM((GROUPS, TILE_ROWS), F32),
            pltpu.VMEM((2, len(SIDE) + 1, GROUPS, TILE_ROWS), BF16),
            pltpu.VMEM((2, len(ARM) + 1, GROUPS, TILE_ROWS), BF16),
            pltpu.VMEM((2, len(FAR) + 1, GROUPS, TILE_ROWS), BF16),
            pltpu.VMEM((NZ, 2 * OWNED, HALF), BF16),
            pltpu.VMEM((2, NM, 2 * OWNED, HALF), BF16),
            pltpu.VMEM((NZ, 2 * OWNED, HALF), BF16),
            pltpu.VMEM((NX, 8, HALF), F32),
            pltpu.VMEM((NY, 8, HALF), F32),
            pltpu.VMEM((NM, 8, HALF), F32),
            dma((2,)),
            dma((2,)),
            dma((2,)),
            dma((2,)),
            dma((2, 3)),
            dma((2, 3)),
            dma((2,)),
            dma((3,)),
            dma((3,)),
            dma((3,)),
            dma((2,)),
            dma((2,)),
            dma((7 + PIECES,)),
        ],
        compiler_params=pltpu.CompilerParams(
            collective_id=0, has_side_effects=True, vmem_limit_bytes=60 * 1024 * 1024
        ),
    )(
        tile_block,
        tile_row,
        order,
        sweeps,
        tiles.reshape(SLOTS, TILE_ROWS, WIDTH),
        labels.reshape(GROUPS, TILE_ROWS),
        weights.reshape(2 * BLOCKS, HALF),
        hess_inv,
    )
    direction, change = pl.pallas_call(
        write_out,
        out_shape=(
            jax.ShapeDtypeStruct((8, HALF), F32),
            jax.ShapeDtypeStruct((GROUPS, TILE_ROWS), F32),
        ),
        in_specs=[vmem] * 2,
        out_specs=[vmem] * 2,
        compiler_params=pltpu.CompilerParams(vmem_limit_bytes=60 * 1024 * 1024),
    )(direction, change)
    return direction.reshape(-1), change.reshape(-1), decrease.reshape(1)


def solution(mesh):
    in_specs = (
        P("feat", ("samp", "rep"), None, None, None),
        P("feat", ("samp", "rep"), None),
        P("feat", ("samp", "rep"), None),
        P(("samp", "rep")),
        P("feat"),
        P(("feat", "samp", "rep"), None, None),
        P("feat", None),
        P("feat"),
    )
    out_specs = (P(("feat", "samp", "rep")), P(("samp", "rep")), P())
    return jax.shard_map(
        on_device, mesh=mesh, in_specs=in_specs, out_specs=out_specs, check_vma=False
    )
```
